32 devices in a mesh: section: 4 (over y, x), dp: 2 (over core), mp: 4 (over z).
Axes of the slice: x: 2, y: 2, z: 4, core: 2. Of those that a mesh axis runs over, the one named last changes fastest.
Arguments:
- cotangent: bfloat16 [256, 4096], P('dp', 'mp'), may hold values from -6 to 6
- saved_inputs: bfloat16 [4, 256, 4096], P('section', 'dp', 'mp'), may hold values from -6 to 6
- pre_acts: bfloat16 [4, 256, 4096], P('section', 'dp', 'mp'), may hold values from -8 to 8
- weights: bfloat16 [4, 4096, 4096], P('section', 'mp', 'dp'), may hold values from -0.046875 to 0.046875
- proj_in: bfloat16 [4, 4096, 64], P('section', 'mp'), may hold values from -0.09375 to 0.09375
- proj_out: bfloat16 [4, 4096, 64], P('section', 'mp'), may hold values from -0.09375 to 0.09375
- query_panels: float32 [4, 4, 4096], P('section', 'dp', 'mp'), may hold values from -4 to 4
- partners: int32 [2, 2], replicated, may hold values from 0 to 1, as said below
Outputs:
- train_panels: float32 [4, 8, 4096], P('section', 'dp', 'mp')
- scores: float32 [4, 2, 4], replicated
The draws below stay inside these ranges and needn't reach their ends.
Inputs may be any that keep to these rules, and one draw needn't show every extreme that they name: The plan has 2 rounds: one round pairs every dp index with itself, and the others are the rounds of one round-robin plan of the 2 indices. The rows of partners hold each of these rounds once, in some order, so partners[r, partners[r, i]] = i.
All inputs are finite; a program needn't handle non-finite values.
Results may differ from the reference program's by a relative error of at most 0.02.
Values may be sent and summed in bfloat16 or wider, within the bound.
A program may use at most 64 MiB of HBM per device.

```python
import math
import jax
import jax.numpy as jnp
from jax import lax

D = 4096
RANK = 64
LEN = 32
EX_DEV = 4
QRY_DEV = 2
SECTIONS = 4
ROUNDS = 2
TRAIN = 8
QUERIES = 4
TOKENS = 256
N_SECTION = 4
N_DP = 2


def draw_partners(key, part):
    first_key, second_key = jax.random.split(jax.random.fold_in(key, 23), 2)
    picks = jax.random.permutation(first_key, N_DP).astype(jnp.int32)
    order = jax.random.permutation(second_key, N_DP).astype(jnp.int32)
    players = jnp.arange(N_DP, dtype=jnp.int32)
    row_list = []
    for round_at in range(ROUNDS):
        pick = picks[round_at]
        which = (pick - 1) % (N_DP - 1)
        other = (2 * which - players) % (N_DP - 1)
        mates = jnp.where(players == N_DP - 1, which, jnp.where(players == which, N_DP - 1, other))
        mates = jnp.where(pick == 0, players, mates)
        labelled = jnp.zeros((N_DP,), jnp.int32).at[order].set(order[mates])
        row_list.append(labelled)
    return jnp.stack(row_list).astype(jnp.int32)


def level_of(own_key, extent, pieces, smallest, high):
    loudness, own = 1.0, jax.random.fold_in(own_key, 6)
    for position, parts in pieces:
        draws = jnp.exp(jax.random.uniform(jax.random.fold_in(own, position), (parts,), jnp.float32, smallest / len(pieces), high / len(pieces)))
        loudness = loudness * jnp.repeat(draws, extent[position] // parts).reshape([-1 if axis == position else 1 for axis in range(len(extent))])
    return loudness


def bell_draw(key, extent, width, bound, shards=(), kind=jnp.bfloat16):
    loudness = level_of(key, extent, shards, -0.22, 0.18) if shards else 1.0
    values = jax.random.normal(key, extent, jnp.float32) * width * loudness
    return jnp.minimum(jnp.maximum(values, -bound), bound).astype(kind)


def setup_inputs(seed: int = 0) -> dict:
    arg_keys = jax.random.split(jax.random.key(seed), 9)
    return {
        "cotangent": bell_draw(arg_keys[0], (TOKENS, D), 1.0, 6.0, ((0, 2), (1, 4))),
        "saved_inputs": bell_draw(arg_keys[1], (SECTIONS, TOKENS, D), 1.0, 6.0, ((0, 4), (1, 2), (2, 4))),
        "pre_acts": bell_draw(arg_keys[2], (SECTIONS, TOKENS, D), 2.0, 8.0, ((0, 4), (1, 2), (2, 4))),
        "weights": bell_draw(arg_keys[3], (SECTIONS, D, D), (4 * D) ** -0.5, 0.046875, ((0, 4), (1, 4), (2, 2))),
        "proj_in": bell_draw(arg_keys[4], (SECTIONS, D, RANK), D ** -0.5, 0.09375, ((0, 4), (1, 4))),
        "proj_out": bell_draw(arg_keys[5], (SECTIONS, D, RANK), D ** -0.5, 0.09375, ((0, 4), (1, 4))),
        "query_panels": bell_draw(arg_keys[6], (SECTIONS, QUERIES, RANK * RANK), 0.5, 4.0, ((0, 4), (1, 2), (2, 4)), jnp.float32),
        "partners": draw_partners(jax.random.fold_in(arg_keys[8], 71), 0),
    }


def silu_slope(pre_state):
    sigma = jax.nn.sigmoid(pre_state)
    return sigma * (1.0 + pre_state * (1.0 - sigma))

def reference(cotangent, saved_inputs, pre_acts, weights, proj_in, proj_out, query_panels, partners):
    delta_grad = cotangent
    panel_list = []
    for layer in reversed(range(N_SECTION)):
        slopes = silu_slope(pre_acts[layer].astype(jnp.float32))
        unit_grad = (delta_grad.astype(jnp.float32) * slopes).astype(jnp.bfloat16)
        in_side = jnp.dot(saved_inputs[layer], proj_in[layer], preferred_element_type=jnp.float32)
        out_side = jnp.dot(unit_grad, proj_out[layer], preferred_element_type=jnp.float32)
        panel_here = jnp.einsum('etr,etc->erc', in_side.reshape(TRAIN, LEN, RANK), out_side.reshape(TRAIN, LEN, RANK), precision=lax.Precision.HIGHEST) / math.sqrt(LEN)
        panel_list.append(panel_here.reshape(TRAIN, RANK * RANK))
        back_term = jnp.dot(unit_grad, weights[layer].T, preferred_element_type=jnp.float32)
        delta_grad = (delta_grad.astype(jnp.float32) + back_term).astype(jnp.bfloat16)
    train_panels = jnp.stack(panel_list[::-1])
    query_view = query_panels.reshape(N_SECTION, N_DP, QRY_DEV, RANK * RANK)
    train_view = train_panels.reshape(N_SECTION, N_DP, EX_DEV, RANK * RANK)
    block_list = []
    for round_at in range(ROUNDS):
        chosen = jnp.take(train_view, partners[round_at].astype(jnp.int32), axis=1)
        block_list.append(jnp.einsum('sbqk,sbek->bqe', query_view, chosen, precision=lax.Precision.HIGHEST))
    stacked = jnp.stack(block_list, axis=1)
    scores = stacked.transpose(0, 2, 1, 3).reshape(QUERIES, ROUNDS, EX_DEV) / (RANK * math.sqrt(N_SECTION))
    return (train_panels, scores)
```

```python
import functools
import math

import jax
import jax.numpy as jnp
from jax import lax
from jax.experimental import pallas as pl
from jax.experimental.pallas import tpu as pltpu
from jax.sharding import PartitionSpec as P

LEN = 32
CHUNK = 16
W_PARTS = 4
MESH = pl.DeviceIdType.MESH


def ring(index, offset, count):
    return lax.rem(index + offset, count)


def pack(block):
    half = block.shape[0] // 2
    return jnp.concatenate([block[:half], block[half:]], axis=1)


def unpack(block):
    half = block.shape[1] // 2
    return jnp.concatenate([block[:, :half], block[:, half:]], axis=0)


def relay_kernel(
    sizes, cot, inputs, pre, weights, proj_in, proj_out, queries, partners,
    panels, table,
    w_full, g_full, d_in, d_out, slope, in_slots, out_slots, in_wide, q_all, p_tiled,
    layer_slots, section_slots, total, result,
    w_here, w_send, w_recv, q_send, q_recv, g_send, g_recv, d_send, d_recv,
    in_send, in_recv, out_send, out_recv, a_send, a_recv, b_send, b_recv, c_send, c_recv,
):
    n_sec, n_dp, n_mp = sizes
    sec = lax.axis_index("section")
    dp = lax.axis_index("dp")
    mp = lax.axis_index("mp")
    tokens, piece = cot.shape
    chunks = tokens // CHUNK
    rank = proj_in.shape[2]
    examples = tokens // LEN
    piece_rank = rank // n_mp
    asked = queries.shape[1]
    rounds = partners.shape[0]
    w_cols = weights.shape[2]
    w_rows = weights.shape[1] // W_PARTS
    top = n_sec - 1
    group = n_dp * n_mp
    here = dp * n_mp + mp

    barrier = pltpu.get_barrier_semaphore()
    for off in range(1, group):
        other = ring(here, off, group)
        pl.semaphore_signal(
            barrier, inc=1,
            device_id={"section": sec, "dp": other // n_mp, "mp": lax.rem(other, n_mp)},
            device_id_type=MESH,
        )
    for off in range(1, n_sec):
        pl.semaphore_signal(
            barrier, inc=1,
            device_id={"section": ring(sec, off, n_sec), "dp": dp, "mp": mp},
            device_id_type=MESH,
        )

    def to(section, dp_at, mp_at, src, dst, send_sem, recv_sem):
        return pltpu.make_async_remote_copy(
            src_ref=src, dst_ref=dst, send_sem=send_sem, recv_sem=recv_sem,
            device_id={"section": section, "dp": dp_at, "mp": mp_at}, device_id_type=MESH,
        )

    my_cols = pl.ds(pl.multiple_of(mp * piece, piece), piece)
    my_w_cols = pl.ds(pl.multiple_of(dp * w_cols, w_cols), w_cols)

    def w_copy(off, part):
        rows = pl.ds(part * w_rows, w_rows)
        return to(sec, ring(dp, off, n_dp), mp, weights.at[0, rows], w_full.at[rows, my_w_cols],
                  w_send.at[off, part], w_recv.at[off, part])

    w_local = pltpu.make_async_copy(weights.at[0], w_full.at[:, my_w_cols], w_here)

    def q_copy(off):
        return to(sec, ring(dp, off, n_dp), mp, queries.at[0], q_all.at[dp],
                  q_send.at[off], q_recv.at[off])

    def g_copy(chunk, off):
        rows = pl.ds(pl.multiple_of(chunk * CHUNK, CHUNK), CHUNK)
        return to(sec, dp, ring(mp, off, n_mp), g_full.at[rows, my_cols], g_full.at[rows, my_cols],
                  g_send.at[chunk, off], g_recv.at[chunk, off])

    def d_copy(chunk):
        rows = pl.ds(pl.multiple_of(chunk * CHUNK, CHUNK), CHUNK)
        return to(lax.rem(sec + n_sec - 1, n_sec), dp, mp, d_out.at[rows], d_in.at[rows],
                  d_send.at[chunk], d_recv.at[chunk])

    def side_copy(slots, off, send, recv):
        return to(sec, dp, ring(mp, off, n_mp), slots.at[0], slots.at[off],
                  send.at[off], recv.at[off])

    def a_copy():
        return to(0, dp, mp, total, layer_slots.at[sec], a_send, a_recv.at[sec])

    def b_copy(off):
        other = ring(here, off, group)
        return to(sec, other // n_mp, lax.rem(other, n_mp), section_slots.at[here],
                  section_slots.at[here], b_send.at[off], b_recv.at[off])

    def c_copy(section):
        return to(section, dp, mp, result, result, c_send.at[section], c_recv)

    @pl.when(sec > 0)
    def _():
        w_local.start()

    slope_pre = pre[0].astype(jnp.float32)
    sigma = 1.0 / (1.0 + jnp.exp(-slope_pre))
    slope[...] = sigma * (1.0 + slope_pre * (1.0 - sigma))

    @pl.when(sec == top)
    def _():
        d_in[...] = cot[...]
        g_full[:, my_cols] = (cot[...].astype(jnp.float32) * slope[...]).astype(jnp.bfloat16)

    pl.semaphore_wait(barrier, group - 1 + n_sec - 1)

    @pl.when(jnp.logical_and(sec == top, sec > 0))
    def _():
        @pl.loop(0, chunks)
        def _(chunk):
            for off in range(1, n_mp):
                g_copy(chunk, off).start()

    @pl.when(sec > 0)
    def _():
        for part in range(W_PARTS):
            for off in range(1, n_dp):
                w_copy(off, part).start()

    q_all[dp] = queries[0]
    for off in range(1, n_dp):
        q_copy(off).start()

    in_slots[0] = pack(jnp.dot(inputs[0], proj_in[0], preferred_element_type=jnp.float32))
    for off in range(1, n_mp):
        side_copy(in_slots, off, in_send, in_recv).start()

    spread = (rank, piece_rank * rank)
    spread_row = lax.broadcasted_iota(jnp.int32, spread, 0)
    spread_col = lax.broadcasted_iota(jnp.int32, spread, 1)
    spread_in = (spread_row == mp * piece_rank + spread_col // rank).astype(jnp.bfloat16)
    spread_out = (spread_row == spread_col % rank).astype(jnp.bfloat16)

    for off in range(1, n_mp):
        side_copy(in_slots, off, in_send, in_recv).wait_recv()
    in_side = in_slots[0]
    for off in range(1, n_mp):
        in_side = in_side + in_slots[off]
    in_side = unpack(in_side) * (1.0 / math.sqrt(LEN))
    in_high = in_side.astype(jnp.bfloat16)
    in_low = (in_side - in_high.astype(jnp.float32)).astype(jnp.bfloat16)
    in_wide[...] = (
        jnp.dot(in_high, spread_in, preferred_element_type=jnp.float32)
        + jnp.dot(in_low, spread_in, preferred_element_type=jnp.float32)
    )

    q_row = lax.broadcasted_iota(jnp.int32, total.shape, 0)
    r_lane = lax.broadcasted_iota(jnp.int32, total.shape, 1)
    mask = jnp.zeros(total.shape, jnp.float32)
    for round_at in range(rounds):
        for index in range(n_dp):
            spot = jnp.logical_and(q_row // asked == index, r_lane // examples == round_at)
            hit = jnp.where(partners[round_at, index] == dp, 1.0, 0.0).astype(jnp.float32)
            mask = mask + jnp.where(spot, hit, 0.0)
    mask = mask * (1.0 / (rank * math.sqrt(n_sec)))
    p_tiled[...] = jnp.zeros_like(p_tiled)

    def step_rows(chunk):
        return pl.ds(pl.multiple_of(chunk * CHUNK, CHUNK), CHUNK)

    def take(chunk):
        rows = step_rows(chunk)
        d_copy(chunk).wait_recv()
        g_full[rows, my_cols] = (
            d_in[rows, :].astype(jnp.float32) * slope[rows, :]
        ).astype(jnp.bfloat16)

    def multiply(chunk):
        rows = step_rows(chunk)
        for off in range(1, n_mp):
            g_copy(chunk, off).wait_recv()
        g_block = g_full[rows, :]
        for part in range(W_PARTS):
            back = lax.dot_general(
                g_block, w_full[part * w_rows:(part + 1) * w_rows, :],
                (((1,), (1,)), ((), ())), preferred_element_type=jnp.float32,
            )
            cols = slice(part * w_rows, (part + 1) * w_rows)
            d_out[rows, cols] = (d_in[rows, cols].astype(jnp.float32) + back).astype(jnp.bfloat16)
        d_copy(chunk).start()

    @pl.when(sec > 0)
    def _():
        w_ready = [w_local.wait]
        for part in range(W_PARTS):
            for off in range(1, n_dp):
                w_ready.append(w_copy(off, part).wait_recv)
        for ready in w_ready:
            ready()

        @pl.loop(0, chunks + 1)
        def _(step):
            @pl.when(jnp.logical_and(sec < top, step < chunks))
            def _():
                take(step)
                for off in range(1, n_mp):
                    g_copy(step, off).start()

            @pl.when(step > 0)
            def _():
                multiply(step - 1)

    @pl.when(jnp.logical_and(sec == 0, sec < top))
    def _():
        @pl.loop(0, chunks)
        def _(step):
            take(step)

    out_slots[0] = pack(
        jnp.dot(g_full[:, my_cols], proj_out[0], preferred_element_type=jnp.float32)
    ).astype(jnp.bfloat16)
    for off in range(1, n_mp):
        side_copy(out_slots, off, out_send, out_recv).start()
    for off in range(1, n_dp):
        q_copy(off).wait_recv()
    for off in range(1, n_mp):
        side_copy(out_slots, off, out_send, out_recv).wait_recv()
    out_side = out_slots[0].astype(jnp.float32)
    for off in range(1, n_mp):
        out_side = out_side + out_slots[off].astype(jnp.float32)
    out_wide = jnp.dot(
        unpack(out_side).astype(jnp.bfloat16), spread_out, preferred_element_type=jnp.float32
    )
    product = in_wide[...] * out_wide
    for example in range(examples):
        row = jnp.sum(product[example * LEN:(example + 1) * LEN], axis=0, keepdims=True)
        panels[0, example:example + 1, :] = row
        for round_at in range(rounds):
            at = round_at * examples + example
            p_tiled[at:at + 1, :] = row
    q_rows = [q_all[index] for index in range(n_dp)]
    pad = total.shape[0] - n_dp * asked
    if pad:
        q_rows.append(jnp.zeros((pad, q_all.shape[2]), jnp.float32))
    share = mask * lax.dot_general(
        jnp.concatenate(q_rows, axis=0), p_tiled[...], (((1,), (1,)), ((), ())),
        precision=lax.Precision.HIGHEST, preferred_element_type=jnp.float32,
    )

    @pl.when(sec > 0)
    def _():
        total[...] = share
        copy = a_copy()
        copy.start()
        copy.wait_send()
        c_copy(sec).wait_recv()

    @pl.when(sec == 0)
    def _():
        summed = share
        for section in range(1, n_sec):
            to(0, dp, mp, total, layer_slots.at[section], a_send, a_recv.at[section]).wait_recv()
            summed = summed + layer_slots[section]
        section_slots[here] = summed
        for off in range(1, group):
            b_copy(off).start()
        for off in range(1, group):
            b_copy(off).wait_recv()
        all_parts = section_slots[0]
        for slot in range(1, group):
            all_parts = all_parts + section_slots[slot]
        result[...] = all_parts
        for section in range(1, n_sec):
            c_copy(section).start()
        for off in range(1, group):
            b_copy(off).wait_send()
        for section in range(1, n_sec):
            c_copy(section).wait_send()

    table[...] = result[...]

    for off in range(1, n_dp):
        q_copy(off).wait_send()
    for off in range(1, n_mp):
        side_copy(in_slots, off, in_send, in_recv).wait_send()
        side_copy(out_slots, off, out_send, out_recv).wait_send()

    @pl.when(sec > 0)
    def _():
        for part in range(W_PARTS):
            for off in range(1, n_dp):
                w_copy(off, part).wait_send()

        @pl.loop(0, chunks)
        def _(chunk):
            for off in range(1, n_mp):
                g_copy(chunk, off).wait_send()
            d_copy(chunk).wait_send()


def body(sizes, cotangent, saved_inputs, pre_acts, weights, proj_in, proj_out, query_panels, partners):
    n_sec, n_dp, n_mp = sizes
    tokens, piece = cotangent.shape
    width = piece * n_mp
    rank = proj_in.shape[2]
    examples = tokens // LEN
    asked = query_panels.shape[1]
    rounds = partners.shape[0]
    chunks = tokens // CHUNK
    panel = query_panels.shape[2]
    q_rows = -(-(n_dp * asked) // 8) * 8
    lanes = 128
    group = n_dp * n_mp
    dma = pltpu.SemaphoreType.DMA
    vmem = pl.BlockSpec(memory_space=pltpu.VMEM)
    panels, table = pl.pallas_call(
        functools.partial(relay_kernel, sizes),
        out_shape=(
            jax.ShapeDtypeStruct((1, examples, panel), jnp.float32),
            jax.ShapeDtypeStruct((q_rows, lanes), jnp.float32),
        ),
        in_specs=[vmem, vmem, vmem, pl.BlockSpec(memory_space=pl.ANY), vmem, vmem, vmem,
                  pl.BlockSpec(memory_space=pltpu.SMEM)],
        out_specs=(vmem, vmem),
        scratch_shapes=[
            pltpu.VMEM((piece, width), jnp.bfloat16),
            pltpu.VMEM((tokens, width), jnp.bfloat16),
            pltpu.VMEM((tokens, piece), jnp.bfloat16),
            pltpu.VMEM((tokens, piece), jnp.bfloat16),
            pltpu.VMEM((tokens, piece), jnp.float32),
            pltpu.VMEM((n_mp, tokens // 2, 2 * rank), jnp.float32),
            pltpu.VMEM((n_mp, tokens // 2, 2 * rank), jnp.bfloat16),
            pltpu.VMEM((tokens, panel), jnp.float32),
            pltpu.VMEM((n_dp, asked, panel), jnp.float32),
            pltpu.VMEM((lanes, panel), jnp.float32),
            pltpu.VMEM((n_sec, q_rows, lanes), jnp.float32),
            pltpu.VMEM((group, q_rows, lanes), jnp.float32),
            pltpu.VMEM((q_rows, lanes), jnp.float32),
            pltpu.VMEM((q_rows, lanes), jnp.float32),
            dma,
            dma((n_dp, W_PARTS)), dma((n_dp, W_PARTS)),
            dma((n_dp,)), dma((n_dp,)),
            dma((chunks, n_mp)), dma((chunks, n_mp)),
            dma((chunks,)), dma((chunks,)),
            dma((n_mp,)), dma((n_mp,)),
            dma((n_mp,)), dma((n_mp,)),
            dma, dma((n_sec,)),
            dma((group,)), dma((group,)),
            dma((n_sec,)), dma,
        ],
        compiler_params=pltpu.CompilerParams(
            collective_id=0, has_side_effects=True, vmem_limit_bytes=40 * 1024 * 1024
        ),
        cost_estimate=pl.CostEstimate(
            flops=2 * tokens * piece * width, bytes_accessed=2 * piece * width, transcendentals=0
        ),
    )(cotangent, saved_inputs, pre_acts, weights, proj_in, proj_out, query_panels, partners)
    scores = table[: n_dp * asked, : rounds * examples].reshape(n_dp * asked, rounds, examples)
    return panels, scores


def solution(mesh):
    placed = (
        P("dp", "mp"),
        P("section", "dp", "mp"),
        P("section", "dp", "mp"),
        P("section", "mp", "dp"),
        P("section", "mp", None),
        P("section", "mp", None),
        P("section", "dp", "mp"),
        P(),
    )
    sizes = (mesh.shape["section"], mesh.shape["dp"], mesh.shape["mp"])
    return jax.shard_map(
        functools.partial(body, sizes), mesh=mesh, in_specs=placed,
        out_specs=(P("section", "dp", "mp"), P()), check_vma=False,
    )
```

```python
import functools
import math

import jax
import jax.numpy as jnp
from jax import lax
from jax.experimental import pallas as pl
from jax.experimental.pallas import tpu as pltpu
from jax.sharding import PartitionSpec as P

LEN = 32
CHUNK = 16
W_PARTS = 4
MESH = pl.DeviceIdType.MESH


def ring(index, offset, count):
    return lax.rem(index + offset, count)


def dot_t(left, right):
    return lax.dot_general(
        left, right, (((1,), (1,)), ((), ())), preferred_element_type=jnp.float32
    )


def pack(block):
    half = block.shape[0] // 2
    return jnp.concatenate([block[:half], block[half:]], axis=1)


def unpack(block):
    half = block.shape[1] // 2
    return jnp.concatenate([block[:, :half], block[:, half:]], axis=0)


def relay_kernel(
    sizes, cot_hbm, inputs_hbm, pre_hbm, weights, proj_in_hbm, proj_out_hbm, queries_hbm, partners,
    panels, table,
    cot, inputs, pre, w_here, proj_in, proj_out, queries,
    g_own, g_all, d_in, d_out, sums_out, sums_in, slope, in_slots, out_slots, in_wide, q_all, p_tiled,
    layer_slots, section_slots, total, result,
    load, q_send, q_recv, g_send, g_recv, d_send, d_recv, s_send, s_recv,
    in_send, in_recv, out_send, out_recv, a_send, a_recv, b_send, b_recv, c_send, c_recv,
):
    n_sec, n_dp, n_mp = sizes
    sec = lax.axis_index("section")
    dp = lax.axis_index("dp")
    mp = lax.axis_index("mp")
    tokens, piece = cot.shape
    loads = [
        pltpu.make_async_copy(src, dst, load.at[at])
        for at, (src, dst) in enumerate((
            (pre_hbm.at[0], pre), (cot_hbm, cot), (inputs_hbm.at[0], inputs),
            (proj_in_hbm.at[0], proj_in), (queries_hbm.at[0], queries),
            (proj_out_hbm.at[0], proj_out), (weights.at[0], w_here),
        ))
    ]
    for copy in loads:
        copy.start()
    load_pre, load_cot, load_inputs, load_in, load_queries, load_out, load_w = loads
    chunks = tokens // CHUNK
    rank = proj_in.shape[0]
    examples = tokens // LEN
    piece_rank = rank // n_mp
    asked = queries.shape[0]
    rounds = partners.shape[0]
    w_cols = w_here.shape[1]
    w_rows = w_here.shape[0] // W_PARTS
    unit = min(piece, w_cols)
    top = n_sec - 1
    group = n_dp * n_mp
    here = dp * n_mp + mp

    barrier = pltpu.get_barrier_semaphore()
    for off in range(1, group):
        other = ring(here, off, group)
        pl.semaphore_signal(
            barrier, inc=1,
            device_id={"section": sec, "dp": other // n_mp, "mp": lax.rem(other, n_mp)},
            device_id_type=MESH,
        )
    for off in range(1, n_sec):
        pl.semaphore_signal(
            barrier, inc=1,
            device_id={"section": ring(sec, off, n_sec), "dp": dp, "mp": mp},
            device_id_type=MESH,
        )

    def to(section, dp_at, mp_at, src, dst, send_sem, recv_sem):
        return pltpu.make_async_remote_copy(
            src_ref=src, dst_ref=dst, send_sem=send_sem, recv_sem=recv_sem,
            device_id={"section": section, "dp": dp_at, "mp": mp_at}, device_id_type=MESH,
        )

    def q_copy(off):
        return to(sec, ring(dp, off, n_dp), mp, queries, q_all.at[dp],
                  q_send.at[off], q_recv.at[off])

    def g_target(sub):
        column = mp * piece + sub * unit
        return column // w_cols, lax.rem(column, w_cols) // unit

    def g_source(at):
        return (dp * w_cols + at * unit) // piece

    def g_spot(chunk, source_dp, at):
        return g_all.at[
            chunk, pl.ds(pl.multiple_of(source_dp * CHUNK, CHUNK), CHUNK),
            pl.ds(pl.multiple_of(at * unit, unit), unit),
        ]

    def g_copy(chunk, sub, off):
        rows = pl.ds(pl.multiple_of(chunk * CHUNK, CHUNK), CHUNK)
        target, at = g_target(sub)
        return to(sec, target, ring(mp, off, n_mp), g_own.at[rows, sub * unit:(sub + 1) * unit],
                  g_spot(chunk, dp, at), g_send.at[chunk, sub, off], g_recv.at[chunk, at, dp])

    def g_move(chunk, act):
        for sub in range(piece // unit):
            target, _ = g_target(sub)
            for off in range(1, n_mp):
                act(g_copy(chunk, sub, off))

            @pl.when(target != dp)
            def _():
                act(g_copy(chunk, sub, 0))

    def g_send_all(chunk):
        g_move(chunk, lambda copy: copy.start())
        rows = pl.ds(pl.multiple_of(chunk * CHUNK, CHUNK), CHUNK)
        for sub in range(piece // unit):
            target, at = g_target(sub)

            @pl.when(target == dp)
            def _():
                g_spot(chunk, dp, at)[...] = g_own[rows, sub * unit:(sub + 1) * unit]

    def g_wait(chunk):
        for at in range(w_cols // unit):
            source = g_source(at)
            for off in range(n_dp):
                source_dp = ring(dp, off, n_dp)

                def wait():
                    spot = g_spot(chunk, source_dp, at)
                    to(sec, dp, source, spot, spot, g_send.at[chunk, 0, 0],
                       g_recv.at[chunk, at, source_dp]).wait_recv()

                if off:
                    wait()
                else:
                    pl.when(source != mp)(wait)

    def s_copy(chunk, off):
        target = ring(dp, off, n_dp)
        return to(sec, target, mp,
                  sums_out.at[chunk, pl.ds(pl.multiple_of(target * CHUNK, CHUNK), CHUNK)],
                  sums_in.at[chunk, off], s_send.at[chunk, off], s_recv.at[chunk, off])

    def d_copy(chunk):
        rows = pl.ds(pl.multiple_of(chunk * CHUNK, CHUNK), CHUNK)
        return to(lax.rem(sec + n_sec - 1, n_sec), dp, mp, d_out.at[rows], d_in.at[rows],
                  d_send.at[chunk], d_recv.at[chunk])

    def side_copy(slots, off, send, recv):
        return to(sec, dp, ring(mp, off, n_mp), slots.at[0], slots.at[off],
                  send.at[off], recv.at[off])

    def a_copy():
        return to(0, dp, mp, total, layer_slots.at[sec], a_send, a_recv.at[sec])

    def b_copy(off):
        other = ring(here, off, group)
        return to(sec, other // n_mp, lax.rem(other, n_mp), section_slots.at[here],
                  section_slots.at[here], b_send.at[off], b_recv.at[off])

    def c_copy(section):
        return to(section, dp, mp, result, result, c_send.at[section], c_recv)

    load_pre.wait()
    slope_pre = pre[...].astype(jnp.float32)
    sigma = 1.0 / (1.0 + jnp.exp(-slope_pre))
    slope[...] = sigma * (1.0 + slope_pre * (1.0 - sigma))
    load_cot.wait()

    @pl.when(sec == top)
    def _():
        d_in[...] = cot[...]
        g_own[...] = (cot[...].astype(jnp.float32) * slope[...]).astype(jnp.bfloat16)

    pl.semaphore_wait(barrier, group - 1 + n_sec - 1)

    @pl.when(jnp.logical_and(sec == top, sec > 0))
    def _():
        @pl.loop(0, chunks)
        def _(chunk):
            g_send_all(chunk)

    load_queries.wait()
    q_all[dp] = queries[...]
    for off in range(1, n_dp):
        q_copy(off).start()

    load_inputs.wait()
    load_in.wait()
    in_slots[0] = pack(dot_t(inputs[...], proj_in[...]))
    for off in range(1, n_mp):
        side_copy(in_slots, off, in_send, in_recv).start()

    spread = (rank, piece_rank * rank)
    spread_row = lax.broadcasted_iota(jnp.int32, spread, 0)
    spread_col = lax.broadcasted_iota(jnp.int32, spread, 1)
    spread_in = (spread_row == mp * piece_rank + spread_col // rank).astype(jnp.bfloat16)
    spread_out = (spread_row == spread_col % rank).astype(jnp.bfloat16)

    for off in range(1, n_mp):
        side_copy(in_slots, off, in_send, in_recv).wait_recv()
    in_side = in_slots[0]
    for off in range(1, n_mp):
        in_side = in_side + in_slots[off]
    in_side = unpack(in_side) * (1.0 / math.sqrt(LEN))
    in_high = in_side.astype(jnp.bfloat16)
    in_low = (in_side - in_high.astype(jnp.float32)).astype(jnp.bfloat16)
    in_wide[...] = (
        jnp.dot(in_high, spread_in, preferred_element_type=jnp.float32)
        + jnp.dot(in_low, spread_in, preferred_element_type=jnp.float32)
    )

    q_row = lax.broadcasted_iota(jnp.int32, total.shape, 0)
    r_lane = lax.broadcasted_iota(jnp.int32, total.shape, 1)
    mask = jnp.zeros(total.shape, jnp.float32)
    for round_at in range(rounds):
        for index in range(n_dp):
            spot = jnp.logical_and(q_row // asked == index, r_lane // examples == round_at)
            hit = jnp.where(partners[round_at, index] == dp, 1.0, 0.0).astype(jnp.float32)
            mask = mask + jnp.where(spot, hit, 0.0)
    mask = mask * (1.0 / (rank * math.sqrt(n_sec)))
    p_tiled[...] = jnp.zeros_like(p_tiled)

    def step_rows(chunk):
        return pl.ds(pl.multiple_of(chunk * CHUNK, CHUNK), CHUNK)

    def take(chunk):
        rows = step_rows(chunk)
        d_copy(chunk).wait_recv()
        g_own[rows, :] = (d_in[rows, :].astype(jnp.float32) * slope[rows, :]).astype(jnp.bfloat16)

    def multiply(chunk):
        rows = step_rows(chunk)
        g_wait(chunk)
        for part in range(W_PARTS):
            cols = slice(part * w_rows, (part + 1) * w_rows)
            sums_out[chunk, :, cols] = dot_t(w_here[cols, :], g_all[chunk]).T
        for off in range(1, n_dp):
            s_copy(chunk, off).start()
        back = sums_out[chunk, pl.ds(pl.multiple_of(dp * CHUNK, CHUNK), CHUNK), :]
        for off in range(1, n_dp):
            s_copy(chunk, off).wait_recv()
            back = back + sums_in[chunk, off]
        d_out[rows, :] = (d_in[rows, :].astype(jnp.float32) + back).astype(jnp.bfloat16)
        d_copy(chunk).start()

    load_w.wait()
    load_out.wait()

    @pl.when(sec > 0)
    def _():
        @pl.loop(0, chunks + 1)
        def _(step):
            @pl.when(jnp.logical_and(sec < top, step < chunks))
            def _():
                take(step)
                g_send_all(step)

            @pl.when(step > 0)
            def _():
                multiply(step - 1)

    @pl.when(jnp.logical_and(sec == 0, sec < top))
    def _():
        @pl.loop(0, chunks)
        def _(step):
            take(step)

    out_slots[0] = pack(dot_t(g_own[...], proj_out[...])).astype(jnp.bfloat16)
    for off in range(1, n_mp):
        side_copy(out_slots, off, out_send, out_recv).start()
    for off in range(1, n_dp):
        q_copy(off).wait_recv()
    for off in range(1, n_mp):
        side_copy(out_slots, off, out_send, out_recv).wait_recv()
    out_side = out_slots[0].astype(jnp.float32)
    for off in range(1, n_mp):
        out_side = out_side + out_slots[off].astype(jnp.float32)
    out_wide = jnp.dot(
        unpack(out_side).astype(jnp.bfloat16), spread_out, preferred_element_type=jnp.float32
    )
    product = in_wide[...] * out_wide
    for example in range(examples):
        row = jnp.sum(product[example * LEN:(example + 1) * LEN], axis=0, keepdims=True)
        panels[0, example:example + 1, :] = row
        for round_at in range(rounds):
            at = round_at * examples + example
            p_tiled[at:at + 1, :] = row
    q_rows = [q_all[index] for index in range(n_dp)]
    pad = total.shape[0] - n_dp * asked
    if pad:
        q_rows.append(jnp.zeros((pad, q_all.shape[2]), jnp.float32))
    share = mask * lax.dot_general(
        jnp.concatenate(q_rows, axis=0), p_tiled[...], (((1,), (1,)), ((), ())),
        precision=lax.Precision.HIGHEST, preferred_element_type=jnp.float32,
    )

    @pl.when(sec > 0)
    def _():
        total[...] = share
        copy = a_copy()
        copy.start()
        copy.wait_send()
        c_copy(sec).wait_recv()

    @pl.when(sec == 0)
    def _():
        summed = share
        for section in range(1, n_sec):
            to(0, dp, mp, total, layer_slots.at[section], a_send, a_recv.at[section]).wait_recv()
            summed = summed + layer_slots[section]
        section_slots[here] = summed
        for off in range(1, group):
            b_copy(off).start()
        for off in range(1, group):
            b_copy(off).wait_recv()
        all_parts = section_slots[0]
        for slot in range(1, group):
            all_parts = all_parts + section_slots[slot]
        result[...] = all_parts
        for section in range(1, n_sec):
            c_copy(section).start()
        for off in range(1, group):
            b_copy(off).wait_send()
        for section in range(1, n_sec):
            c_copy(section).wait_send()

    table[...] = result[...]

    for off in range(1, n_dp):
        q_copy(off).wait_send()
    for off in range(1, n_mp):
        side_copy(in_slots, off, in_send, in_recv).wait_send()
        side_copy(out_slots, off, out_send, out_recv).wait_send()

    @pl.when(sec > 0)
    def _():
        @pl.loop(0, chunks)
        def _(chunk):
            g_move(chunk, lambda copy: copy.wait_send())
            for off in range(1, n_dp):
                s_copy(chunk, off).wait_send()
            d_copy(chunk).wait_send()


def body(sizes, cotangent, saved_inputs, pre_acts, weights, proj_in, proj_out, query_panels, partners):
    n_sec, n_dp, n_mp = sizes
    tokens, piece = cotangent.shape
    width = piece * n_mp
    w_cols = weights.shape[2]
    unit = min(piece, w_cols)
    rank = proj_in.shape[2]
    examples = tokens // LEN
    asked = query_panels.shape[1]
    rounds = partners.shape[0]
    chunks = tokens // CHUNK
    panel = query_panels.shape[2]
    q_rows = -(-(n_dp * asked) // 8) * 8
    lanes = 128
    group = n_dp * n_mp
    dma = pltpu.SemaphoreType.DMA
    vmem = pl.BlockSpec(memory_space=pltpu.VMEM)
    hbm = pl.BlockSpec(memory_space=pltpu.HBM)
    panels, table = pl.pallas_call(
        functools.partial(relay_kernel, sizes),
        out_shape=(
            jax.ShapeDtypeStruct((1, examples, panel), jnp.float32),
            jax.ShapeDtypeStruct((q_rows, lanes), jnp.float32),
        ),
        in_specs=[hbm] * 7 + [pl.BlockSpec(memory_space=pltpu.SMEM)],
        out_specs=(vmem, vmem),
        scratch_shapes=[
            pltpu.VMEM((tokens, piece), jnp.bfloat16),
            pltpu.VMEM((tokens, piece), jnp.bfloat16),
            pltpu.VMEM((tokens, piece), jnp.bfloat16),
            pltpu.VMEM((piece, w_cols), jnp.bfloat16),
            pltpu.VMEM((rank, piece), jnp.bfloat16),
            pltpu.VMEM((rank, piece), jnp.bfloat16),
            pltpu.VMEM((asked, panel), jnp.float32),
            pltpu.VMEM((tokens, piece), jnp.bfloat16),
            pltpu.VMEM((chunks, n_dp * CHUNK, w_cols), jnp.bfloat16),
            pltpu.VMEM((tokens, piece), jnp.bfloat16),
            pltpu.VMEM((tokens, piece), jnp.bfloat16),
            pltpu.VMEM((chunks, n_dp * CHUNK, piece), jnp.float32),
            pltpu.VMEM((chunks, n_dp, CHUNK, piece), jnp.float32),
            pltpu.VMEM((tokens, piece), jnp.float32),
            pltpu.VMEM((n_mp, tokens // 2, 2 * rank), jnp.float32),
            pltpu.VMEM((n_mp, tokens // 2, 2 * rank), jnp.bfloat16),
            pltpu.VMEM((tokens, panel), jnp.float32),
            pltpu.VMEM((n_dp, asked, panel), jnp.float32),
            pltpu.VMEM((lanes, panel), jnp.float32),
            pltpu.VMEM((n_sec, q_rows, lanes), jnp.float32),
            pltpu.VMEM((group, q_rows, lanes), jnp.float32),
            pltpu.VMEM((q_rows, lanes), jnp.float32),
            pltpu.VMEM((q_rows, lanes), jnp.float32),
            dma((7,)),
            dma((n_dp,)), dma((n_dp,)),
            dma((chunks, piece // unit, n_mp)), dma((chunks, w_cols // unit, n_dp)),
            dma((chunks,)), dma((chunks,)),
            dma((chunks, n_dp)), dma((chunks, n_dp)),
            dma((n_mp,)), dma((n_mp,)),
            dma((n_mp,)), dma((n_mp,)),
            dma, dma((n_sec,)),
            dma((group,)), dma((group,)),
            dma((n_sec,)), dma,
        ],
        compiler_params=pltpu.CompilerParams(
            collective_id=0, has_side_effects=True, vmem_limit_bytes=64 * 1024 * 1024
        ),
        cost_estimate=pl.CostEstimate(
            flops=2 * tokens * piece * width, bytes_accessed=2 * piece * w_cols, transcendentals=0
        ),
    )(cotangent, saved_inputs, pre_acts, weights, jnp.swapaxes(proj_in, 1, 2),
      jnp.swapaxes(proj_out, 1, 2), query_panels, partners)
    scores = table[: n_dp * asked, : rounds * examples].reshape(n_dp * asked, rounds, examples)
    return panels, scores


def solution(mesh):
    placed = (
        P("dp", "mp"),
        P("section", "dp", "mp"),
        P("section", "dp", "mp"),
        P("section", "mp", "dp"),
        P("section", "mp", None),
        P("section", "mp", None),
        P("section", "dp", "mp"),
        P(),
    )
    sizes = (mesh.shape["section"], mesh.shape["dp"], mesh.shape["mp"])
    return jax.shard_map(
        functools.partial(body, sizes), mesh=mesh, in_specs=placed,
        out_specs=(P("section", "dp", "mp"), P()), check_vma=False,
    )
```

```python
import functools
import math

import jax
import jax.numpy as jnp
from jax import lax
from jax.experimental import pallas as pl
from jax.experimental.pallas import tpu as pltpu
from jax.sharding import PartitionSpec as P

LEN = 32
CHUNK = 16
W_PARTS = 4
MESH = pl.DeviceIdType.MESH


def ring(index, offset, count):
    return lax.rem(index + offset, count)


def dot_t(left, right):
    return lax.dot_general(
        left, right, (((1,), (1,)), ((), ())), preferred_element_type=jnp.float32
    )


def pack(block):
    half = block.shape[0] // 2
    return jnp.concatenate([block[:half], block[half:]], axis=1)


def unpack(block):
    half = block.shape[1] // 2
    return jnp.concatenate([block[:, :half], block[:, half:]], axis=0)


def relay_kernel(
    sizes, cot_hbm, inputs_hbm, pre_hbm, weights, proj_in_hbm, proj_out_hbm, queries_hbm, partners,
    panels, table,
    cot, inputs, pre, w_here, proj_in, proj_out, queries,
    g_own, g_all, d_in, d_out, sums_out, sums_in, slope, in_slots, out_slots, in_wide, q_all, p_tiled,
    layer_slots, section_slots, total, result,
    load, q_send, q_recv, g_send, g_recv, d_send, d_recv, s_send, s_recv,
    in_send, in_recv, out_send, out_recv, a_send, a_recv, b_send, b_recv, c_send, c_recv,
):
    n_sec, n_dp, n_mp = sizes
    sec = lax.axis_index("section")
    dp = lax.axis_index("dp")
    mp = lax.axis_index("mp")
    tokens, piece = cot.shape
    loads = [
        pltpu.make_async_copy(src, dst, load.at[at])
        for at, (src, dst) in enumerate((
            (pre_hbm.at[0], pre), (cot_hbm, cot), (inputs_hbm.at[0], inputs),
            (proj_in_hbm.at[0], proj_in), (queries_hbm.at[0], queries),
            (proj_out_hbm.at[0], proj_out), (weights.at[0], w_here),
        ))
    ]
    for copy in loads:
        copy.start()
    load_pre, load_cot, load_inputs, load_in, load_queries, load_out, load_w = loads
    chunks = tokens // CHUNK
    rank = proj_in.shape[0]
    examples = tokens // LEN
    piece_rank = rank // n_mp
    asked = queries.shape[0]
    rounds = partners.shape[0]
    w_cols = w_here.shape[1]
    w_rows = w_here.shape[0] // W_PARTS
    unit = min(piece, w_cols)
    top = n_sec - 1
    group = n_dp * n_mp
    here = dp * n_mp + mp

    barrier = pltpu.get_barrier_semaphore()
    for off in range(1, group):
        other = ring(here, off, group)
        pl.semaphore_signal(
            barrier, inc=1,
            device_id={"section": sec, "dp": other // n_mp, "mp": lax.rem(other, n_mp)},
            device_id_type=MESH,
        )
    for off in range(1, n_sec):
        pl.semaphore_signal(
            barrier, inc=1,
            device_id={"section": ring(sec, off, n_sec), "dp": dp, "mp": mp},
            device_id_type=MESH,
        )

    def to(section, dp_at, mp_at, src, dst, send_sem, recv_sem):
        return pltpu.make_async_remote_copy(
            src_ref=src, dst_ref=dst, send_sem=send_sem, recv_sem=recv_sem,
            device_id={"section": section, "dp": dp_at, "mp": mp_at}, device_id_type=MESH,
        )

    def q_copy(off):
        return to(sec, ring(dp, off, n_dp), mp, queries, q_all.at[dp],
                  q_send.at[off], q_recv.at[off])

    def g_target(sub):
        column = mp * piece + sub * unit
        return column // w_cols, lax.rem(column, w_cols) // unit

    def g_source(at):
        return (dp * w_cols + at * unit) // piece

    def g_spot(chunk, source_dp, at):
        return g_all.at[
            chunk, pl.ds(pl.multiple_of(source_dp * CHUNK, CHUNK), CHUNK),
            pl.ds(pl.multiple_of(at * unit, unit), unit),
        ]

    def g_copy(chunk, sub, off):
        rows = pl.ds(pl.multiple_of(chunk * CHUNK, CHUNK), CHUNK)
        target, at = g_target(sub)
        return to(sec, target, ring(mp, off, n_mp), g_own.at[rows, sub * unit:(sub + 1) * unit],
                  g_spot(chunk, dp, at), g_send.at[chunk, sub, off], g_recv.at[chunk, at, dp])

    def g_move(chunk, act):
        for sub in range(piece // unit):
            target, _ = g_target(sub)
            for off in range(1, n_mp):
                act(g_copy(chunk, sub, off))

            @pl.when(target != dp)
            def _():
                act(g_copy(chunk, sub, 0))

    def g_send_all(chunk):
        g_move(chunk, lambda copy: copy.start())
        rows = pl.ds(pl.multiple_of(chunk * CHUNK, CHUNK), CHUNK)
        for sub in range(piece // unit):
            target, at = g_target(sub)

            @pl.when(target == dp)
            def _():
                g_spot(chunk, dp, at)[...] = g_own[rows, sub * unit:(sub + 1) * unit]

    def g_wait(chunk):
        for at in range(w_cols // unit):
            source = g_source(at)
            for off in range(n_dp):
                source_dp = ring(dp, off, n_dp)

                def wait():
                    spot = g_spot(chunk, source_dp, at)
                    to(sec, dp, source, spot, spot, g_send.at[chunk, 0, 0],
                       g_recv.at[chunk, at, source_dp]).wait_recv()

                if off:
                    wait()
                else:
                    pl.when(source != mp)(wait)

    def s_copy(chunk, off):
        target = ring(dp, off, n_dp)
        return to(sec, target, mp,
                  sums_out.at[chunk, pl.ds(pl.multiple_of(target * CHUNK, CHUNK), CHUNK)],
                  sums_in.at[chunk, off], s_send.at[chunk, off], s_recv.at[chunk, off])

    def d_copy(chunk):
        rows = pl.ds(pl.multiple_of(chunk * CHUNK, CHUNK), CHUNK)
        return to(lax.rem(sec + n_sec - 1, n_sec), dp, mp, d_out.at[rows], d_in.at[rows],
                  d_send.at[chunk], d_recv.at[chunk])

    def side_copy(slots, off, send, recv):
        return to(sec, dp, ring(mp, off, n_mp), slots.at[0], slots.at[off],
                  send.at[off], recv.at[off])

    def a_copy():
        return to(0, dp, mp, total, layer_slots.at[sec], a_send, a_recv.at[sec])

    def b_copy(off):
        other = ring(here, off, group)
        return to(sec, other // n_mp, lax.rem(other, n_mp), section_slots.at[here],
                  section_slots.at[here], b_send.at[off], b_recv.at[off])

    def c_copy(section):
        return to(section, dp, mp, result, result, c_send.at[section], c_recv)

    load_pre.wait()
    slope_pre = pre[...].astype(jnp.float32)
    sigma = 1.0 / (1.0 + jnp.exp(-slope_pre))
    slope[...] = sigma * (1.0 + slope_pre * (1.0 - sigma))
    load_cot.wait()

    @pl.when(sec == top)
    def _():
        d_in[...] = cot[...]
        g_own[...] = (cot[...].astype(jnp.float32) * slope[...]).astype(jnp.bfloat16)

    pl.semaphore_wait(barrier, group - 1 + n_sec - 1)

    load_queries.wait()
    q_all[dp] = queries[...]
    for off in range(1, n_dp):
        q_copy(off).start()

    load_inputs.wait()
    load_in.wait()
    in_slots[0] = pack(dot_t(inputs[...], proj_in[...]))
    for off in range(1, n_mp):
        side_copy(in_slots, off, in_send, in_recv).start()

    spread = (rank, piece_rank * rank)
    spread_row = lax.broadcasted_iota(jnp.int32, spread, 0)
    spread_col = lax.broadcasted_iota(jnp.int32, spread, 1)
    spread_in = (spread_row == mp * piece_rank + spread_col // rank).astype(jnp.bfloat16)
    spread_out = (spread_row == spread_col % rank).astype(jnp.bfloat16)

    for off in range(1, n_mp):
        side_copy(in_slots, off, in_send, in_recv).wait_recv()
    in_side = in_slots[0]
    for off in range(1, n_mp):
        in_side = in_side + in_slots[off]
    in_side = unpack(in_side) * (1.0 / math.sqrt(LEN))
    in_high = in_side.astype(jnp.bfloat16)
    in_low = (in_side - in_high.astype(jnp.float32)).astype(jnp.bfloat16)
    in_wide[...] = (
        jnp.dot(in_high, spread_in, preferred_element_type=jnp.float32)
        + jnp.dot(in_low, spread_in, preferred_element_type=jnp.float32)
    )

    q_row = lax.broadcasted_iota(jnp.int32, total.shape, 0)
    r_lane = lax.broadcasted_iota(jnp.int32, total.shape, 1)
    mask = jnp.zeros(total.shape, jnp.float32)
    for round_at in range(rounds):
        for index in range(n_dp):
            spot = jnp.logical_and(q_row // asked == index, r_lane // examples == round_at)
            hit = jnp.where(partners[round_at, index] == dp, 1.0, 0.0).astype(jnp.float32)
            mask = mask + jnp.where(spot, hit, 0.0)
    mask = mask * (1.0 / (rank * math.sqrt(n_sec)))
    p_tiled[...] = jnp.zeros_like(p_tiled)

    def step_rows(chunk):
        return pl.ds(pl.multiple_of(chunk * CHUNK, CHUNK), CHUNK)

    def take(chunk):
        rows = step_rows(chunk)
        d_copy(chunk).wait_recv()
        g_own[rows, :] = (d_in[rows, :].astype(jnp.float32) * slope[rows, :]).astype(jnp.bfloat16)

    def multiply(chunk):
        rows = step_rows(chunk)
        g_wait(chunk)
        for part in range(W_PARTS):
            cols = slice(part * w_rows, (part + 1) * w_rows)
            sums_out[chunk, :, cols] = dot_t(w_here[cols, :], g_all[chunk]).T
        for off in range(1, n_dp):
            s_copy(chunk, off).start()
        back = sums_out[chunk, pl.ds(pl.multiple_of(dp * CHUNK, CHUNK), CHUNK), :]
        for off in range(1, n_dp):
            s_copy(chunk, off).wait_recv()
            back = back + sums_in[chunk, off]
        d_out[rows, :] = (d_in[rows, :].astype(jnp.float32) + back).astype(jnp.bfloat16)
        d_copy(chunk).start()

    load_w.wait()
    load_out.wait()

    @pl.when(sec > 0)
    def _():
        @pl.loop(0, chunks + 1)
        def _(step):
            @pl.when(step < chunks)
            def _():
                @pl.when(sec < top)
                def _():
                    take(step)

                g_send_all(step)

            @pl.when(step > 0)
            def _():
                multiply(step - 1)

    @pl.when(jnp.logical_and(sec == 0, sec < top))
    def _():
        @pl.loop(0, chunks)
        def _(step):
            take(step)

    out_slots[0] = pack(dot_t(g_own[...], proj_out[...])).astype(jnp.bfloat16)
    for off in range(1, n_mp):
        side_copy(out_slots, off, out_send, out_recv).start()
    for off in range(1, n_dp):
        q_copy(off).wait_recv()
    for off in range(1, n_mp):
        side_copy(out_slots, off, out_send, out_recv).wait_recv()
    out_side = out_slots[0].astype(jnp.float32)
    for off in range(1, n_mp):
        out_side = out_side + out_slots[off].astype(jnp.float32)
    out_wide = jnp.dot(
        unpack(out_side).astype(jnp.bfloat16), spread_out, preferred_element_type=jnp.float32
    )
    product = in_wide[...] * out_wide
    for example in range(examples):
        row = jnp.sum(product[example * LEN:(example + 1) * LEN], axis=0, keepdims=True)
        panels[0, example:example + 1, :] = row
        for round_at in range(rounds):
            at = round_at * examples + example
            p_tiled[at:at + 1, :] = row
    q_rows = [q_all[index] for index in range(n_dp)]
    pad = total.shape[0] - n_dp * asked
    if pad:
        q_rows.append(jnp.zeros((pad, q_all.shape[2]), jnp.float32))
    share = mask * lax.dot_general(
        jnp.concatenate(q_rows, axis=0), p_tiled[...], (((1,), (1,)), ((), ())),
        precision=lax.Precision.HIGHEST, preferred_element_type=jnp.float32,
    )

    @pl.when(sec > 0)
    def _():
        total[...] = share
        copy = a_copy()
        copy.start()
        copy.wait_send()
        c_copy(sec).wait_recv()

    @pl.when(sec == 0)
    def _():
        summed = share
        for section in range(1, n_sec):
            to(0, dp, mp, total, layer_slots.at[section], a_send, a_recv.at[section]).wait_recv()
            summed = summed + layer_slots[section]
        section_slots[here] = summed
        for off in range(1, group):
            b_copy(off).start()
        for off in range(1, group):
            b_copy(off).wait_recv()
        all_parts = section_slots[0]
        for slot in range(1, group):
            all_parts = all_parts + section_slots[slot]
        result[...] = all_parts
        for section in range(1, n_sec):
            c_copy(section).start()
        for off in range(1, group):
            b_copy(off).wait_send()
        for section in range(1, n_sec):
            c_copy(section).wait_send()

    for query in range(n_dp * asked):
        for round_at in range(rounds):
            table[query, round_at:round_at + 1, :] = result[
                query:query + 1, round_at * examples:(round_at + 1) * examples
            ]

    for off in range(1, n_dp):
        q_copy(off).wait_send()
    for off in range(1, n_mp):
        side_copy(in_slots, off, in_send, in_recv).wait_send()
        side_copy(out_slots, off, out_send, out_recv).wait_send()

    @pl.when(sec > 0)
    def _():
        @pl.loop(0, chunks)
        def _(chunk):
            g_move(chunk, lambda copy: copy.wait_send())
            for off in range(1, n_dp):
                s_copy(chunk, off).wait_send()
            d_copy(chunk).wait_send()


def body(sizes, cotangent, saved_inputs, pre_acts, weights, proj_in, proj_out, query_panels, partners):
    n_sec, n_dp, n_mp = sizes
    tokens, piece = cotangent.shape
    width = piece * n_mp
    w_cols = weights.shape[2]
    unit = min(piece, w_cols)
    rank = proj_in.shape[2]
    examples = tokens // LEN
    asked = query_panels.shape[1]
    rounds = partners.shape[0]
    chunks = tokens // CHUNK
    panel = query_panels.shape[2]
    q_rows = -(-(n_dp * asked) // 8) * 8
    lanes = 128
    group = n_dp * n_mp
    dma = pltpu.SemaphoreType.DMA
    vmem = pl.BlockSpec(memory_space=pltpu.VMEM)
    hbm = pl.BlockSpec(memory_space=pltpu.HBM)
    return pl.pallas_call(
        functools.partial(relay_kernel, sizes),
        out_shape=(
            jax.ShapeDtypeStruct((1, examples, panel), jnp.float32),
            jax.ShapeDtypeStruct((n_dp * asked, rounds, examples), jnp.float32),
        ),
        in_specs=[hbm] * 7 + [pl.BlockSpec(memory_space=pltpu.SMEM)],
        out_specs=(vmem, vmem),
        scratch_shapes=[
            pltpu.VMEM((tokens, piece), jnp.bfloat16),
            pltpu.VMEM((tokens, piece), jnp.bfloat16),
            pltpu.VMEM((tokens, piece), jnp.bfloat16),
            pltpu.VMEM((piece, w_cols), jnp.bfloat16),
            pltpu.VMEM((rank, piece), jnp.bfloat16),
            pltpu.VMEM((rank, piece), jnp.bfloat16),
            pltpu.VMEM((asked, panel), jnp.float32),
            pltpu.VMEM((tokens, piece), jnp.bfloat16),
            pltpu.VMEM((chunks, n_dp * CHUNK, w_cols), jnp.bfloat16),
            pltpu.VMEM((tokens, piece), jnp.bfloat16),
            pltpu.VMEM((tokens, piece), jnp.bfloat16),
            pltpu.VMEM((chunks, n_dp * CHUNK, piece), jnp.float32),
            pltpu.VMEM((chunks, n_dp, CHUNK, piece), jnp.float32),
            pltpu.VMEM((tokens, piece), jnp.float32),
            pltpu.VMEM((n_mp, tokens // 2, 2 * rank), jnp.float32),
            pltpu.VMEM((n_mp, tokens // 2, 2 * rank), jnp.bfloat16),
            pltpu.VMEM((tokens, panel), jnp.float32),
            pltpu.VMEM((n_dp, asked, panel), jnp.float32),
            pltpu.VMEM((lanes, panel), jnp.float32),
            pltpu.VMEM((n_sec, q_rows, lanes), jnp.float32),
            pltpu.VMEM((group, q_rows, lanes), jnp.float32),
            pltpu.VMEM((q_rows, lanes), jnp.float32),
            pltpu.VMEM((q_rows, lanes), jnp.float32),
            dma((7,)),
            dma((n_dp,)), dma((n_dp,)),
            dma((chunks, piece // unit, n_mp)), dma((chunks, w_cols // unit, n_dp)),
            dma((chunks,)), dma((chunks,)),
            dma((chunks, n_dp)), dma((chunks, n_dp)),
            dma((n_mp,)), dma((n_mp,)),
            dma((n_mp,)), dma((n_mp,)),
            dma, dma((n_sec,)),
            dma((group,)), dma((group,)),
            dma((n_sec,)), dma,
        ],
        compiler_params=pltpu.CompilerParams(
            collective_id=0, has_side_effects=True, vmem_limit_bytes=64 * 1024 * 1024
        ),
        cost_estimate=pl.CostEstimate(
            flops=2 * tokens * piece * width, bytes_accessed=2 * piece * w_cols, transcendentals=0
        ),
    )(cotangent, saved_inputs, pre_acts, weights, jnp.swapaxes(proj_in, 1, 2),
      jnp.swapaxes(proj_out, 1, 2), query_panels, partners)


def solution(mesh):
    placed = (
        P("dp", "mp"),
        P("section", "dp", "mp"),
        P("section", "dp", "mp"),
        P("section", "mp", "dp"),
        P("section", "mp", None),
        P("section", "mp", None),
        P("section", "dp", "mp"),
        P(),
    )
    sizes = (mesh.shape["section"], mesh.shape["dp"], mesh.shape["mp"])
    return jax.shard_map(
        functools.partial(body, sizes), mesh=mesh, in_specs=placed,
        out_specs=(P("section", "dp", "mp"), P()), check_vma=False,
    )
```

```python
import functools
import math

import jax
import jax.numpy as jnp
from jax import lax
from jax.experimental import pallas as pl
from jax.experimental.pallas import tpu as pltpu
from jax.sharding import PartitionSpec as P

LEN = 32
CHUNK = 32
W_PARTS = 4
MESH = pl.DeviceIdType.MESH


def ring(index, offset, count):
    return lax.rem(index + offset, count)


def dot_t(left, right):
    return lax.dot_general(
        left, right, (((1,), (1,)), ((), ())), preferred_element_type=jnp.float32
    )


def pack(block):
    half = block.shape[0] // 2
    return jnp.concatenate([block[:half], block[half:]], axis=1)


def unpack(block):
    half = block.shape[1] // 2
    return jnp.concatenate([block[:, :half], block[:, half:]], axis=0)


def relay_kernel(
    sizes, cot_hbm, inputs_hbm, pre_hbm, weights, proj_in_hbm, proj_out_hbm, queries_hbm, partners,
    panels, table,
    cot, inputs, pre, w_here, proj_in, proj_out, queries,
    g_own, g_all, d_in, d_out, sums_out, sums_in, slope, in_slots, out_slots, in_wide, q_all, p_tiled,
    layer_slots, section_slots, total, result,
    load, q_send, q_recv, g_send, g_recv, d_send, d_recv, s_send, s_recv,
    in_send, in_recv, out_send, out_recv, a_send, a_recv, b_send, b_recv, c_send, c_recv,
):
    n_sec, n_dp, n_mp = sizes
    sec = lax.axis_index("section")
    dp = lax.axis_index("dp")
    mp = lax.axis_index("mp")
    tokens, piece = cot.shape
    loads = [
        pltpu.make_async_copy(src, dst, load.at[at])
        for at, (src, dst) in enumerate((
            (pre_hbm.at[0], pre), (cot_hbm, cot), (inputs_hbm.at[0], inputs),
            (proj_in_hbm.at[0], proj_in), (queries_hbm.at[0], queries),
            (proj_out_hbm.at[0], proj_out), (weights.at[0], w_here),
        ))
    ]
    for copy in loads:
        copy.start()
    load_pre, load_cot, load_inputs, load_in, load_queries, load_out, load_w = loads
    chunks = tokens // CHUNK
    rank = proj_in.shape[0]
    examples = tokens // LEN
    piece_rank = rank // n_mp
    asked = queries.shape[0]
    rounds = partners.shape[0]
    w_cols = w_here.shape[1]
    w_rows = w_here.shape[0] // W_PARTS
    unit = min(piece, w_cols)
    top = n_sec - 1
    group = n_dp * n_mp
    here = dp * n_mp + mp

    barrier = pltpu.get_barrier_semaphore()
    for off in range(1, group):
        other = ring(here, off, group)
        pl.semaphore_signal(
            barrier, inc=1,
            device_id={"section": sec, "dp": other // n_mp, "mp": lax.rem(other, n_mp)},
            device_id_type=MESH,
        )
    for off in range(1, n_sec):
        pl.semaphore_signal(
            barrier, inc=1,
            device_id={"section": ring(sec, off, n_sec), "dp": dp, "mp": mp},
            device_id_type=MESH,
        )

    def to(section, dp_at, mp_at, src, dst, send_sem, recv_sem):
        return pltpu.make_async_remote_copy(
            src_ref=src, dst_ref=dst, send_sem=send_sem, recv_sem=recv_sem,
            device_id={"section": section, "dp": dp_at, "mp": mp_at}, device_id_type=MESH,
        )

    def q_copy(off):
        return to(sec, ring(dp, off, n_dp), mp, queries, q_all.at[dp],
                  q_send.at[off], q_recv.at[off])

    def g_target(sub):
        column = mp * piece + sub * unit
        return column // w_cols, lax.rem(column, w_cols) // unit

    def g_source(at):
        return (dp * w_cols + at * unit) // piece

    def g_spot(chunk, source_dp, at):
        return g_all.at[
            chunk, pl.ds(pl.multiple_of(source_dp * CHUNK, CHUNK), CHUNK),
            pl.ds(pl.multiple_of(at * unit, unit), unit),
        ]

    def g_copy(chunk, sub, off):
        rows = pl.ds(pl.multiple_of(chunk * CHUNK, CHUNK), CHUNK)
        target, at = g_target(sub)
        return to(sec, target, ring(mp, off, n_mp), g_own.at[rows, sub * unit:(sub + 1) * unit],
                  g_spot(chunk, dp, at), g_send.at[chunk, sub, off], g_recv.at[chunk, at, dp])

    def g_move(chunk, act):
        for sub in range(piece // unit):
            target, _ = g_target(sub)
            for off in range(1, n_mp):
                act(g_copy(chunk, sub, off))

            @pl.when(target != dp)
            def _():
                act(g_copy(chunk, sub, 0))

    def g_send_all(chunk):
        g_move(chunk, lambda copy: copy.start())
        rows = pl.ds(pl.multiple_of(chunk * CHUNK, CHUNK), CHUNK)
        for sub in range(piece // unit):
            target, at = g_target(sub)

            @pl.when(target == dp)
            def _():
                g_spot(chunk, dp, at)[...] = g_own[rows, sub * unit:(sub + 1) * unit]

    def g_wait(chunk):
        for at in range(w_cols // unit):
            source = g_source(at)
            for off in range(n_dp):
                source_dp = ring(dp, off, n_dp)

                def wait():
                    spot = g_spot(chunk, source_dp, at)
                    to(sec, dp, source, spot, spot, g_send.at[chunk, 0, 0],
                       g_recv.at[chunk, at, source_dp]).wait_recv()

                if off:
                    wait()
                else:
                    pl.when(source != mp)(wait)

    def s_copy(chunk, off):
        target = ring(dp, off, n_dp)
        return to(sec, target, mp,
                  sums_out.at[chunk, pl.ds(pl.multiple_of(target * CHUNK, CHUNK), CHUNK)],
                  sums_in.at[chunk, off], s_send.at[chunk, off], s_recv.at[chunk, off])

    def d_copy(chunk):
        rows = pl.ds(pl.multiple_of(chunk * CHUNK, CHUNK), CHUNK)
        return to(lax.rem(sec + n_sec - 1, n_sec), dp, mp, d_out.at[rows], d_in.at[rows],
                  d_send.at[chunk], d_recv.at[chunk])

    def side_copy(slots, off, send, recv):
        return to(sec, dp, ring(mp, off, n_mp), slots.at[0], slots.at[off],
                  send.at[off], recv.at[off])

    def a_copy():
        return to(0, dp, mp, total, layer_slots.at[sec], a_send, a_recv.at[sec])

    def b_copy(off):
        other = ring(here, off, group)
        return to(sec, other // n_mp, lax.rem(other, n_mp), section_slots.at[here],
                  section_slots.at[here], b_send.at[off], b_recv.at[off])

    def c_copy(section):
        return to(section, dp, mp, result, result, c_send.at[section], c_recv)

    load_pre.wait()
    slope_pre = pre[...].astype(jnp.float32)
    sigma = 1.0 / (1.0 + jnp.exp(-slope_pre))
    slope[...] = sigma * (1.0 + slope_pre * (1.0 - sigma))
    load_cot.wait()

    @pl.when(sec == top)
    def _():
        d_in[...] = cot[...]
        g_own[...] = (cot[...].astype(jnp.float32) * slope[...]).astype(jnp.bfloat16)

    pl.semaphore_wait(barrier, group - 1 + n_sec - 1)

    load_queries.wait()
    q_all[dp] = queries[...]
    for off in range(1, n_dp):
        q_copy(off).start()

    load_inputs.wait()
    load_in.wait()
    in_slots[0] = pack(dot_t(inputs[...], proj_in[...]))
    for off in range(1, n_mp):
        side_copy(in_slots, off, in_send, in_recv).start()

    spread = (rank, piece_rank * rank)
    spread_row = lax.broadcasted_iota(jnp.int32, spread, 0)
    spread_col = lax.broadcasted_iota(jnp.int32, spread, 1)
    spread_in = (spread_row == mp * piece_rank + spread_col // rank).astype(jnp.bfloat16)
    spread_out = (spread_row == spread_col % rank).astype(jnp.bfloat16)

    for off in range(1, n_mp):
        side_copy(in_slots, off, in_send, in_recv).wait_recv()
    in_side = in_slots[0]
    for off in range(1, n_mp):
        in_side = in_side + in_slots[off]
    in_side = unpack(in_side) * (1.0 / math.sqrt(LEN))
    in_high = in_side.astype(jnp.bfloat16)
    in_low = (in_side - in_high.astype(jnp.float32)).astype(jnp.bfloat16)
    in_wide[...] = (
        jnp.dot(in_high, spread_in, preferred_element_type=jnp.float32)
        + jnp.dot(in_low, spread_in, preferred_element_type=jnp.float32)
    )

    q_row = lax.broadcasted_iota(jnp.int32, total.shape, 0)
    r_lane = lax.broadcasted_iota(jnp.int32, total.shape, 1)
    mask = jnp.zeros(total.shape, jnp.float32)
    for round_at in range(rounds):
        for index in range(n_dp):
            spot = jnp.logical_and(q_row // asked == index, r_lane // examples == round_at)
            hit = jnp.where(partners[round_at, index] == dp, 1.0, 0.0).astype(jnp.float32)
            mask = mask + jnp.where(spot, hit, 0.0)
    mask = mask * (1.0 / (rank * math.sqrt(n_sec)))
    p_tiled[...] = jnp.zeros_like(p_tiled)

    def step_rows(chunk):
        return pl.ds(pl.multiple_of(chunk * CHUNK, CHUNK), CHUNK)

    def take(chunk):
        rows = step_rows(chunk)
        d_copy(chunk).wait_recv()
        g_own[rows, :] = (d_in[rows, :].astype(jnp.float32) * slope[rows, :]).astype(jnp.bfloat16)

    def multiply(chunk):
        rows = step_rows(chunk)
        g_wait(chunk)
        for part in range(W_PARTS):
            cols = slice(part * w_rows, (part + 1) * w_rows)
            sums_out[chunk, :, cols] = dot_t(w_here[cols, :], g_all[chunk]).T
        for off in range(1, n_dp):
            s_copy(chunk, off).start()
        back = sums_out[chunk, pl.ds(pl.multiple_of(dp * CHUNK, CHUNK), CHUNK), :]
        for off in range(1, n_dp):
            s_copy(chunk, off).wait_recv()
            back = back + sums_in[chunk, off]
        d_out[rows, :] = (d_in[rows, :].astype(jnp.float32) + back).astype(jnp.bfloat16)
        d_copy(chunk).start()

    load_w.wait()
    load_out.wait()

    @pl.when(sec > 0)
    def _():
        @pl.loop(0, chunks + 1)
        def _(step):
            @pl.when(step < chunks)
            def _():
                @pl.when(sec < top)
                def _():
                    take(step)

                g_send_all(step)

            @pl.when(step > 0)
            def _():
                multiply(step - 1)

    @pl.when(jnp.logical_and(sec == 0, sec < top))
    def _():
        @pl.loop(0, chunks)
        def _(step):
            take(step)

    out_slots[0] = pack(dot_t(g_own[...], proj_out[...])).astype(jnp.bfloat16)
    for off in range(1, n_mp):
        side_copy(out_slots, off, out_send, out_recv).start()
    for off in range(1, n_dp):
        q_copy(off).wait_recv()
    for off in range(1, n_mp):
        side_copy(out_slots, off, out_send, out_recv).wait_recv()
    out_side = out_slots[0].astype(jnp.float32)
    for off in range(1, n_mp):
        out_side = out_side + out_slots[off].astype(jnp.float32)
    out_wide = jnp.dot(
        unpack(out_side).astype(jnp.bfloat16), spread_out, preferred_element_type=jnp.float32
    )
    product = in_wide[...] * out_wide
    for example in range(examples):
        row = jnp.sum(product[example * LEN:(example + 1) * LEN], axis=0, keepdims=True)
        panels[0, example:example + 1, :] = row
        for round_at in range(rounds):
            at = round_at * examples + example
            p_tiled[at:at + 1, :] = row
    q_rows = [q_all[index] for index in range(n_dp)]
    pad = total.shape[0] - n_dp * asked
    if pad:
        q_rows.append(jnp.zeros((pad, q_all.shape[2]), jnp.float32))
    share = mask * lax.dot_general(
        jnp.concatenate(q_rows, axis=0), p_tiled[...], (((1,), (1,)), ((), ())),
        precision=lax.Precision.HIGHEST, preferred_element_type=jnp.float32,
    )

    @pl.when(sec > 0)
    def _():
        total[...] = share
        copy = a_copy()
        copy.start()
        copy.wait_send()
        c_copy(sec).wait_recv()

    @pl.when(sec == 0)
    def _():
        summed = share
        for section in range(1, n_sec):
            to(0, dp, mp, total, layer_slots.at[section], a_send, a_recv.at[section]).wait_recv()
            summed = summed + layer_slots[section]
        section_slots[here] = summed
        for off in range(1, group):
            b_copy(off).start()
        for off in range(1, group):
            b_copy(off).wait_recv()
        all_parts = section_slots[0]
        for slot in range(1, group):
            all_parts = all_parts + section_slots[slot]
        result[...] = all_parts
        for section in range(1, n_sec):
            c_copy(section).start()
        for off in range(1, group):
            b_copy(off).wait_send()
        for section in range(1, n_sec):
            c_copy(section).wait_send()

    for query in range(n_dp * asked):
        for round_at in range(rounds):
            table[query, round_at:round_at + 1, :] = result[
                query:query + 1, round_at * examples:(round_at + 1) * examples
            ]

    for off in range(1, n_dp):
        q_copy(off).wait_send()
    for off in range(1, n_mp):
        side_copy(in_slots, off, in_send, in_recv).wait_send()
        side_copy(out_slots, off, out_send, out_recv).wait_send()

    @pl.when(sec > 0)
    def _():
        @pl.loop(0, chunks)
        def _(chunk):
            g_move(chunk, lambda copy: copy.wait_send())
            for off in range(1, n_dp):
                s_copy(chunk, off).wait_send()
            d_copy(chunk).wait_send()


def body(sizes, cotangent, saved_inputs, pre_acts, weights, proj_in, proj_out, query_panels, partners):
    n_sec, n_dp, n_mp = sizes
    tokens, piece = cotangent.shape
    width = piece * n_mp
    w_cols = weights.shape[2]
    unit = min(piece, w_cols)
    rank = proj_in.shape[2]
    examples = tokens // LEN
    asked = query_panels.shape[1]
    rounds = partners.shape[0]
    chunks = tokens // CHUNK
    panel = query_panels.shape[2]
    q_rows = -(-(n_dp * asked) // 8) * 8
    lanes = 128
    group = n_dp * n_mp
    dma = pltpu.SemaphoreType.DMA
    vmem = pl.BlockSpec(memory_space=pltpu.VMEM)
    hbm = pl.BlockSpec(memory_space=pltpu.HBM)
    return pl.pallas_call(
        functools.partial(relay_kernel, sizes),
        out_shape=(
            jax.ShapeDtypeStruct((1, examples, panel), jnp.float32),
            jax.ShapeDtypeStruct((n_dp * asked, rounds, examples), jnp.float32),
        ),
        in_specs=[hbm] * 7 + [pl.BlockSpec(memory_space=pltpu.SMEM)],
        out_specs=(vmem, vmem),
        scratch_shapes=[
            pltpu.VMEM((tokens, piece), jnp.bfloat16),
            pltpu.VMEM((tokens, piece), jnp.bfloat16),
            pltpu.VMEM((tokens, piece), jnp.bfloat16),
            pltpu.VMEM((piece, w_cols), jnp.bfloat16),
            pltpu.VMEM((rank, piece), jnp.bfloat16),
            pltpu.VMEM((rank, piece), jnp.bfloat16),
            pltpu.VMEM((asked, panel), jnp.float32),
            pltpu.VMEM((tokens, piece), jnp.bfloat16),
            pltpu.VMEM((chunks, n_dp * CHUNK, w_cols), jnp.bfloat16),
            pltpu.VMEM((tokens, piece), jnp.bfloat16),
            pltpu.VMEM((tokens, piece), jnp.bfloat16),
            pltpu.VMEM((chunks, n_dp * CHUNK, piece), jnp.float32),
            pltpu.VMEM((chunks, n_dp, CHUNK, piece), jnp.float32),
            pltpu.VMEM((tokens, piece), jnp.float32),
            pltpu.VMEM((n_mp, tokens // 2, 2 * rank), jnp.float32),
            pltpu.VMEM((n_mp, tokens // 2, 2 * rank), jnp.bfloat16),
            pltpu.VMEM((tokens, panel), jnp.float32),
            pltpu.VMEM((n_dp, asked, panel), jnp.float32),
            pltpu.VMEM((lanes, panel), jnp.float32),
            pltpu.VMEM((n_sec, q_rows, lanes), jnp.float32),
            pltpu.VMEM((group, q_rows, lanes), jnp.float32),
            pltpu.VMEM((q_rows, lanes), jnp.float32),
            pltpu.VMEM((q_rows, lanes), jnp.float32),
            dma((7,)),
            dma((n_dp,)), dma((n_dp,)),
            dma((chunks, piece // unit, n_mp)), dma((chunks, w_cols // unit, n_dp)),
            dma((chunks,)), dma((chunks,)),
            dma((chunks, n_dp)), dma((chunks, n_dp)),
            dma((n_mp,)), dma((n_mp,)),
            dma((n_mp,)), dma((n_mp,)),
            dma, dma((n_sec,)),
            dma((group,)), dma((group,)),
            dma((n_sec,)), dma,
        ],
        compiler_params=pltpu.CompilerParams(
            collective_id=0, has_side_effects=True, vmem_limit_bytes=64 * 1024 * 1024
        ),
        cost_estimate=pl.CostEstimate(
            flops=2 * tokens * piece * width, bytes_accessed=2 * piece * w_cols, transcendentals=0
        ),
    )(cotangent, saved_inputs, pre_acts, weights, jnp.swapaxes(proj_in, 1, 2),
      jnp.swapaxes(proj_out, 1, 2), query_panels, partners)


def solution(mesh):
    placed = (
        P("dp", "mp"),
        P("section", "dp", "mp"),
        P("section", "dp", "mp"),
        P("section", "mp", "dp"),
        P("section", "mp", None),
        P("section", "mp", None),
        P("section", "dp", "mp"),
        P(),
    )
    sizes = (mesh.shape["section"], mesh.shape["dp"], mesh.shape["mp"])
    return jax.shard_map(
        functools.partial(body, sizes), mesh=mesh, in_specs=placed,
        out_specs=(P("section", "dp", "mp"), P()), check_vma=False,
    )
```

```python
import functools
import math

import jax
import jax.numpy as jnp
from jax import lax
from jax.experimental import pallas as pl
from jax.experimental.pallas import tpu as pltpu
from jax.sharding import PartitionSpec as P

LEN = 32
CHUNK = 16
W_PARTS = 4
MESH = pl.DeviceIdType.MESH


def ring(index, offset, count):
    return lax.rem(index + offset, count)


def dot_t(left, right):
    return lax.dot_general(
        left, right, (((1,), (1,)), ((), ())), preferred_element_type=jnp.float32
    )


def pack(block):
    half = block.shape[0] // 2
    return jnp.concatenate([block[:half], block[half:]], axis=1)


def unpack(block):
    half = block.shape[1] // 2
    return jnp.concatenate([block[:, :half], block[:, half:]], axis=0)


def relay_kernel(
    sizes, cot_hbm, inputs_hbm, pre_hbm, weights, proj_in_hbm, proj_out_hbm, queries_hbm, partners,
    panels, table,
    cot, inputs, pre, w_here, proj_in, proj_wide, queries,
    g_own, g_all, d_in, d_out, sums_out, sums_in, slope, in_slots, out_slots, in_wide, q_all, q_pad, spread_out, mask,
    layer_slots, section_slots, total, result,
    load, q_send, q_recv, g_send, g_recv, f_send, d_send, d_recv, s_send, s_recv,
    in_send, in_recv, out_send, out_recv, a_send, a_recv, b_send, b_recv, c_send, c_recv,
):
    n_sec, n_dp, n_mp = sizes
    sec = lax.axis_index("section")
    dp = lax.axis_index("dp")
    mp = lax.axis_index("mp")
    tokens, piece = cot.shape
    loads = [
        pltpu.make_async_copy(src, dst, load.at[at])
        for at, (src, dst) in enumerate((
            (pre_hbm.at[0], pre), (cot_hbm, cot), (inputs_hbm.at[0], inputs),
            (proj_in_hbm.at[0], proj_in), (queries_hbm.at[0], queries),
            (proj_out_hbm.at[0], proj_wide.at[pl.ds(0, proj_out_hbm.shape[1])]), (weights.at[0], w_here),
        ))
    ]
    for copy in loads:
        copy.start()
    load_pre, load_cot, load_inputs, load_in, load_queries, load_out, load_w = loads
    chunks = tokens // CHUNK
    rank = proj_in.shape[0]
    examples = tokens // LEN
    piece_rank = rank // n_mp
    asked = queries.shape[0]
    rounds = partners.shape[0]
    w_cols = w_here.shape[1]
    w_rows = w_here.shape[0] // W_PARTS
    unit = min(piece, w_cols)
    top = n_sec - 1
    group = n_dp * n_mp
    here = dp * n_mp + mp

    barrier = pltpu.get_barrier_semaphore()
    for off in range(1, group):
        other = ring(here, off, group)
        pl.semaphore_signal(
            barrier, inc=1,
            device_id={"section": sec, "dp": other // n_mp, "mp": lax.rem(other, n_mp)},
            device_id_type=MESH,
        )
    for off in range(1, n_sec):
        pl.semaphore_signal(
            barrier, inc=1,
            device_id={"section": ring(sec, off, n_sec), "dp": dp, "mp": mp},
            device_id_type=MESH,
        )

    def to(section, dp_at, mp_at, src, dst, send_sem, recv_sem):
        return pltpu.make_async_remote_copy(
            src_ref=src, dst_ref=dst, send_sem=send_sem, recv_sem=recv_sem,
            device_id={"section": section, "dp": dp_at, "mp": mp_at}, device_id_type=MESH,
        )

    def q_copy(off):
        return to(sec, ring(dp, off, n_dp), mp, queries, q_all.at[dp],
                  q_send.at[off], q_recv.at[off])

    def g_target(sub):
        column = mp * piece + sub * unit
        return column // w_cols, lax.rem(column, w_cols) // unit

    def g_source(at):
        return (dp * w_cols + at * unit) // piece

    def g_spot(chunk, source_dp, at):
        return g_all.at[
            chunk, pl.ds(pl.multiple_of(source_dp * CHUNK, CHUNK), CHUNK),
            pl.ds(pl.multiple_of(at * unit, unit), unit),
        ]

    def g_copy(chunk, sub, off):
        rows = pl.ds(pl.multiple_of(chunk * CHUNK, CHUNK), CHUNK)
        target, at = g_target(sub)
        return to(sec, target, ring(mp, off, n_mp), g_own.at[rows, sub * unit:(sub + 1) * unit],
                  g_spot(chunk, dp, at), g_send.at[chunk, sub, off], g_recv.at[chunk, at, dp])

    def g_move(chunk, act):
        for sub in range(piece // unit):
            target, _ = g_target(sub)
            for off in range(1, n_mp):
                if n_mp == 4 and off != 2:
                    pl.when(mp != (0 if off == 3 else 3))(
                        functools.partial(act, g_copy(chunk, sub, off))
                    )
                else:
                    act(g_copy(chunk, sub, off))

            @pl.when(target != dp)
            def _():
                act(g_copy(chunk, sub, 0))

    def g_send_all(chunk):
        g_move(chunk, lambda copy: copy.start())
        rows = pl.ds(pl.multiple_of(chunk * CHUNK, CHUNK), CHUNK)
        for sub in range(piece // unit):
            target, at = g_target(sub)

            @pl.when(target == dp)
            def _():
                g_spot(chunk, dp, at)[...] = g_own[rows, sub * unit:(sub + 1) * unit]

    def g_arrival(chunk, source_dp, at):
        spot = g_spot(chunk, source_dp, at)
        return to(sec, dp, mp, spot, spot, g_send.at[chunk, 0, 0], g_recv.at[chunk, at, source_dp])

    def forwards(source):
        return jnp.logical_or(
            jnp.logical_and(source == 0, mp == 2), jnp.logical_and(source == 3, mp == 1)
        )

    def f_copy(chunk, source_dp, at):
        spot = g_spot(chunk, source_dp, at)
        return to(sec, dp, jnp.where(mp == 2, 3, 0), spot, spot,
                  f_send.at[chunk, at, source_dp], g_recv.at[chunk, at, source_dp])

    def forward(chunk, wait_send=False):
        if n_mp != 4:
            return
        for at in range(w_cols // unit):
            @pl.when(forwards(g_source(at)))
            def _():
                for off in range(n_dp):
                    source_dp = ring(dp, off, n_dp)
                    if wait_send:
                        f_copy(chunk, source_dp, at).wait_send()
                    else:
                        g_arrival(chunk, source_dp, at).wait_recv()
                        f_copy(chunk, source_dp, at).start()

    def g_wait(chunk):
        for at in range(w_cols // unit):
            source = g_source(at)
            for off in range(n_dp):
                source_dp = ring(dp, off, n_dp)
                expected = source != mp if off == 0 else source >= 0
                if n_mp == 4:
                    expected = jnp.logical_and(expected, jnp.logical_not(forwards(source)))

                @pl.when(expected)
                def _():
                    g_arrival(chunk, source_dp, at).wait_recv()

    def s_copy(chunk, off):
        target = ring(dp, off, n_dp)
        return to(sec, target, mp,
                  sums_out.at[chunk, pl.ds(pl.multiple_of(target * CHUNK, CHUNK), CHUNK)],
                  sums_in.at[chunk, off], s_send.at[chunk, off], s_recv.at[chunk, off])

    def d_copy(chunk):
        rows = pl.ds(pl.multiple_of(chunk * CHUNK, CHUNK), CHUNK)
        return to(lax.rem(sec + n_sec - 1, n_sec), dp, mp, d_out.at[rows], d_in.at[rows],
                  d_send.at[chunk], d_recv.at[chunk])

    def in_copy(off):
        return to(sec, dp, ring(mp, off, n_mp), in_slots.at[0], in_slots.at[off],
                  in_send.at[off], in_recv.at[off])

    def out_copy(chunk, off):
        return to(sec, dp, ring(mp, off, n_mp), out_slots.at[0, chunk], out_slots.at[off, chunk],
                  out_send.at[chunk, off], out_recv.at[chunk, off])

    def a_copy():
        return to(0, dp, mp, total, layer_slots.at[sec], a_send, a_recv.at[sec])

    def b_copy(off):
        other = ring(here, off, group)
        return to(sec, other // n_mp, lax.rem(other, n_mp), section_slots.at[here],
                  section_slots.at[here], b_send.at[off], b_recv.at[off])

    def c_copy(section):
        return to(section, dp, mp, result, result, c_send.at[section], c_recv)

    load_pre.wait()
    slope_pre = pre[...].astype(jnp.float32)
    sigma = 1.0 / (1.0 + jnp.exp(-slope_pre))
    slope[...] = sigma * (1.0 + slope_pre * (1.0 - sigma))
    load_cot.wait()

    @pl.when(sec == top)
    def _():
        d_in[...] = cot[...]
        g_own[...] = (cot[...].astype(jnp.float32) * slope[...]).astype(jnp.bfloat16)

    pl.semaphore_wait(barrier, group - 1 + n_sec - 1)

    q_row = lax.broadcasted_iota(jnp.int32, total.shape, 0)
    r_lane = lax.broadcasted_iota(jnp.int32, total.shape, 1)

    def prepare():
        load_queries.wait()
        q_all[dp] = queries[...]
        for off in range(1, n_dp):
            q_copy(off).start()

        load_inputs.wait()
        load_in.wait()
        in_slots[0] = pack(dot_t(inputs[...], proj_in[...]))
        for off in range(1, n_mp):
            in_copy(off).start()

        spread = spread_out.shape
        spread_row = lax.broadcasted_iota(jnp.int32, spread, 0)
        spread_col = lax.broadcasted_iota(jnp.int32, spread, 1)
        spread_out[...] = (spread_row == spread_col % rank).astype(jnp.bfloat16)
        spread_in = (
            spread_row[:rank] == mp * piece_rank + spread_col[:rank] // rank
        ).astype(jnp.bfloat16)

        chosen = jnp.zeros(total.shape, jnp.float32)
        for round_at in range(rounds):
            for index in range(n_dp):
                spot = jnp.logical_and(q_row // asked == index, r_lane // examples == round_at)
                hit = jnp.where(partners[round_at, index] == dp, 1.0, 0.0).astype(jnp.float32)
                chosen = chosen + jnp.where(spot, hit, 0.0)
        mask[...] = chosen * (1.0 / (rank * math.sqrt(n_sec)))
        total[...] = jnp.zeros_like(total)

        q_pad[...] = jnp.zeros_like(q_pad)
        for off in range(1, n_dp):
            q_copy(off).wait_recv()
        for index in range(n_dp):
            q_pad[index * asked:(index + 1) * asked, :] = q_all[index]

        for off in range(1, n_mp):
            in_copy(off).wait_recv()
        in_side = in_slots[0]
        for off in range(1, n_mp):
            in_side = in_side + in_slots[off]
        in_side = unpack(in_side) * (1.0 / math.sqrt(LEN))
        in_high = in_side.astype(jnp.bfloat16)
        in_low = (in_side - in_high.astype(jnp.float32)).astype(jnp.bfloat16)
        in_wide[...] = (
            jnp.dot(in_high, spread_in, preferred_element_type=jnp.float32)
            + jnp.dot(in_low, spread_in, preferred_element_type=jnp.float32)
        )

    def step_rows(chunk):
        return pl.ds(pl.multiple_of(chunk * CHUNK, CHUNK), CHUNK)

    def take(chunk):
        rows = step_rows(chunk)
        d_copy(chunk).wait_recv()
        g_own[rows, :] = (d_in[rows, :].astype(jnp.float32) * slope[rows, :]).astype(jnp.bfloat16)

    def multiply(chunk):
        rows = step_rows(chunk)
        g_wait(chunk)
        for part in range(W_PARTS):
            cols = slice(part * w_rows, (part + 1) * w_rows)
            sums_out[chunk, :, cols] = dot_t(w_here[cols, :], g_all[chunk]).T
        for off in range(1, n_dp):
            s_copy(chunk, off).start()
        back = sums_out[chunk, pl.ds(pl.multiple_of(dp * CHUNK, CHUNK), CHUNK), :]
        for off in range(1, n_dp):
            s_copy(chunk, off).wait_recv()
            back = back + sums_in[chunk, off]
        d_out[rows, :] = (d_in[rows, :].astype(jnp.float32) + back).astype(jnp.bfloat16)
        d_copy(chunk).start()

    def project(chunk):
        out_slots[0, chunk] = dot_t(g_own[step_rows(chunk), :], proj_wide[...]).astype(jnp.bfloat16)
        for off in range(1, n_mp):
            out_copy(chunk, off).start()

    per = LEN // CHUNK

    def panel(example):
        out_side = jnp.zeros((LEN, out_slots.shape[3]), jnp.float32)
        for off in range(n_mp):
            if off:
                for at in range(per):
                    out_copy(example * per + at, off).wait_recv()
            block = out_slots[off, pl.ds(example * per, per)].astype(jnp.float32)
            out_side = out_side + block.reshape(out_side.shape)
        out_wide = jnp.dot(
            out_side.astype(jnp.bfloat16), spread_out[...], preferred_element_type=jnp.float32
        )
        rows = pl.ds(pl.multiple_of(example * LEN, LEN), LEN)
        row = jnp.sum(in_wide[rows, :] * out_wide, axis=0, keepdims=True)
        panels[0, pl.ds(example, 1), :] = row
        column = jnp.sum(q_pad[...] * row, axis=1, keepdims=True)
        total[...] += jnp.where(lax.rem(r_lane, examples) == example, column, 0.0)

    proj_wide[rank:, :] = jnp.zeros((proj_wide.shape[0] - rank, piece), jnp.bfloat16)
    load_out.wait()
    pl.when(sec < top)(prepare)
    load_w.wait()

    @pl.when(sec > 0)
    def _():
        @pl.loop(0, chunks + 1)
        def _(step):
            @pl.when(jnp.logical_and(sec == top, step < chunks))
            def _():
                g_send_all(step)
                project(step)

            @pl.when(step > 0)
            def _():
                forward(step - 1)

            @pl.when(jnp.logical_and(sec < top, step < chunks))
            def _():
                take(step)
                g_send_all(step)
                project(step)

            @pl.when(step > 0)
            def _():
                multiply(step - 1)

        pl.when(sec == top)(prepare)

        @pl.loop(0, examples)
        def _(example):
            panel(example)

    @pl.when(sec == 0)
    def _():
        @pl.loop(0, chunks)
        def _(step):
            take(step)
            project(step)

            @pl.when(jnp.logical_and(lax.rem(step, per) == per - 1, step >= 2 * per - 1))
            def _():
                panel(step // per - 1)

        panel(examples - 1)

    share = total[...] * mask[...]

    @pl.when(sec > 0)
    def _():
        total[...] = share
        copy = a_copy()
        copy.start()
        copy.wait_send()
        c_copy(sec).wait_recv()

    @pl.when(sec == 0)
    def _():
        summed = share
        for section in range(1, n_sec):
            to(0, dp, mp, total, layer_slots.at[section], a_send, a_recv.at[section]).wait_recv()
            summed = summed + layer_slots[section]
        section_slots[here] = summed
        for off in range(1, group):
            b_copy(off).start()
        for off in range(1, group):
            b_copy(off).wait_recv()
        all_parts = section_slots[0]
        for slot in range(1, group):
            all_parts = all_parts + section_slots[slot]
        result[...] = all_parts
        for section in range(1, n_sec):
            c_copy(section).start()
        for off in range(1, group):
            b_copy(off).wait_send()
        for section in range(1, n_sec):
            c_copy(section).wait_send()

    for query in range(n_dp * asked):
        for round_at in range(rounds):
            table[query, round_at:round_at + 1, :] = result[
                query:query + 1, round_at * examples:(round_at + 1) * examples
            ]

    for off in range(1, n_dp):
        q_copy(off).wait_send()
    for off in range(1, n_mp):
        in_copy(off).wait_send()

    @pl.loop(0, chunks)
    def _(chunk):
        for off in range(1, n_mp):
            out_copy(chunk, off).wait_send()

    @pl.when(sec > 0)
    def _():
        @pl.loop(0, chunks)
        def _(chunk):
            g_move(chunk, lambda copy: copy.wait_send())
            forward(chunk, wait_send=True)
            for off in range(1, n_dp):
                s_copy(chunk, off).wait_send()
            d_copy(chunk).wait_send()


def body(sizes, cotangent, saved_inputs, pre_acts, weights, proj_in, proj_out, query_panels, partners):
    n_sec, n_dp, n_mp = sizes
    tokens, piece = cotangent.shape
    width = piece * n_mp
    w_cols = weights.shape[2]
    unit = min(piece, w_cols)
    rank = proj_in.shape[2]
    examples = tokens // LEN
    asked = query_panels.shape[1]
    rounds = partners.shape[0]
    chunks = tokens // CHUNK
    panel = query_panels.shape[2]
    q_rows = -(-(n_dp * asked) // 8) * 8
    lanes = 128
    group = n_dp * n_mp
    dma = pltpu.SemaphoreType.DMA
    vmem = pl.BlockSpec(memory_space=pltpu.VMEM)
    hbm = pl.BlockSpec(memory_space=pltpu.HBM)
    return pl.pallas_call(
        functools.partial(relay_kernel, sizes),
        out_shape=(
            jax.ShapeDtypeStruct((1, examples, panel), jnp.float32),
            jax.ShapeDtypeStruct((n_dp * asked, rounds, examples), jnp.float32),
        ),
        in_specs=[hbm] * 7 + [pl.BlockSpec(memory_space=pltpu.SMEM)],
        out_specs=(vmem, vmem),
        scratch_shapes=[
            pltpu.VMEM((tokens, piece), jnp.bfloat16),
            pltpu.VMEM((tokens, piece), jnp.bfloat16),
            pltpu.VMEM((tokens, piece), jnp.bfloat16),
            pltpu.VMEM((piece, w_cols), jnp.bfloat16),
            pltpu.VMEM((rank, piece), jnp.bfloat16),
            pltpu.VMEM((2 * rank, piece), jnp.bfloat16),
            pltpu.VMEM((asked, panel), jnp.float32),
            pltpu.VMEM((tokens, piece), jnp.bfloat16),
            pltpu.VMEM((chunks, n_dp * CHUNK, w_cols), jnp.bfloat16),
            pltpu.VMEM((tokens, piece), jnp.bfloat16),
            pltpu.VMEM((tokens, piece), jnp.bfloat16),
            pltpu.VMEM((chunks, n_dp * CHUNK, piece), jnp.float32),
            pltpu.VMEM((chunks, n_dp, CHUNK, piece), jnp.float32),
            pltpu.VMEM((tokens, piece), jnp.float32),
            pltpu.VMEM((n_mp, tokens // 2, 2 * rank), jnp.float32),
            pltpu.VMEM((n_mp, chunks, CHUNK, 2 * rank), jnp.bfloat16),
            pltpu.VMEM((tokens, panel), jnp.float32),
            pltpu.VMEM((n_dp, asked, panel), jnp.float32),
            pltpu.VMEM((q_rows, panel), jnp.float32),
            pltpu.VMEM((2 * rank, panel), jnp.bfloat16),
            pltpu.VMEM((q_rows, lanes), jnp.float32),
            pltpu.VMEM((n_sec, q_rows, lanes), jnp.float32),
            pltpu.VMEM((group, q_rows, lanes), jnp.float32),
            pltpu.VMEM((q_rows, lanes), jnp.float32),
            pltpu.VMEM((q_rows, lanes), jnp.float32),
            dma((7,)),
            dma((n_dp,)), dma((n_dp,)),
            dma((chunks, piece // unit, n_mp)), dma((chunks, w_cols // unit, n_dp)),
            dma((chunks, w_cols // unit, n_dp)),
            dma((chunks,)), dma((chunks,)),
            dma((chunks, n_dp)), dma((chunks, n_dp)),
            dma((n_mp,)), dma((n_mp,)),
            dma((chunks, n_mp)), dma((chunks, n_mp)),
            dma, dma((n_sec,)),
            dma((group,)), dma((group,)),
            dma((n_sec,)), dma,
        ],
        compiler_params=pltpu.CompilerParams(
            collective_id=0, has_side_effects=True, vmem_limit_bytes=64 * 1024 * 1024
        ),
        cost_estimate=pl.CostEstimate(
            flops=2 * tokens * piece * width, bytes_accessed=2 * piece * w_cols, transcendentals=0
        ),
    )(cotangent, saved_inputs, pre_acts, weights, jnp.swapaxes(proj_in, 1, 2),
      jnp.swapaxes(proj_out, 1, 2), query_panels, partners)


def solution(mesh):
    placed = (
        P("dp", "mp"),
        P("section", "dp", "mp"),
        P("section", "dp", "mp"),
        P("section", "mp", "dp"),
        P("section", "mp", None),
        P("section", "mp", None),
        P("section", "dp", "mp"),
        P(),
    )
    sizes = (mesh.shape["section"], mesh.shape["dp"], mesh.shape["mp"])
    return jax.shard_map(
        functools.partial(body, sizes), mesh=mesh, in_specs=placed,
        out_specs=(P("section", "dp", "mp"), P()), check_vma=False,
    )
```

```python
import functools
import math

import jax
import jax.numpy as jnp
from jax import lax
from jax.experimental import pallas as pl
from jax.experimental.pallas import tpu as pltpu
from jax.sharding import PartitionSpec as P

LEN = 32
CHUNK = 16
W_PARTS = 4
MESH = pl.DeviceIdType.MESH


def ring(index, offset, count):
    return lax.rem(index + offset, count)


def dot_t(left, right):
    return lax.dot_general(
        left, right, (((1,), (1,)), ((), ())), preferred_element_type=jnp.float32
    )


def pack(block):
    half = block.shape[0] // 2
    return jnp.concatenate([block[:half], block[half:]], axis=1)


def unpack(block):
    half = block.shape[1] // 2
    return jnp.concatenate([block[:, :half], block[:, half:]], axis=0)


def relay_kernel(
    sizes, cot_hbm, inputs_hbm, pre_hbm, weights, proj_in_hbm, proj_out_hbm, queries_hbm, partners,
    panels, table,
    cot, inputs, pre, w_here, proj_in, proj_wide, queries,
    g_own, g_all, d_in, d_out, sums_out, sums_in, slope, in_slots, out_slots, in_wide, q_all, q_pad, spread_out, mask,
    layer_slots, section_slots, total, result,
    load, q_send, q_recv, g_send, g_recv, d_send, d_recv, s_send, s_recv,
    in_send, in_recv, out_send, out_recv, a_send, a_recv, b_send, b_recv, c_send, c_recv,
):
    n_sec, n_dp, n_mp = sizes
    sec = lax.axis_index("section")
    dp = lax.axis_index("dp")
    mp = lax.axis_index("mp")
    tokens, piece = cot.shape
    loads = [
        pltpu.make_async_copy(src, dst, load.at[at])
        for at, (src, dst) in enumerate((
            (pre_hbm.at[0], pre), (cot_hbm, cot), (inputs_hbm.at[0], inputs),
            (proj_in_hbm.at[0], proj_in), (queries_hbm.at[0], queries),
            (proj_out_hbm.at[0], proj_wide.at[pl.ds(0, proj_out_hbm.shape[1])]), (weights.at[0], w_here),
        ))
    ]
    for copy in loads:
        copy.start()
    load_pre, load_cot, load_inputs, load_in, load_queries, load_out, load_w = loads
    chunks = tokens // CHUNK
    rank = proj_in.shape[0]
    examples = tokens // LEN
    piece_rank = rank // n_mp
    asked = queries.shape[0]
    rounds = partners.shape[0]
    w_cols = w_here.shape[1]
    w_rows = w_here.shape[0] // W_PARTS
    unit = min(piece, w_cols)
    top = n_sec - 1
    group = n_dp * n_mp
    here = dp * n_mp + mp

    barrier = pltpu.get_barrier_semaphore()
    for off in range(1, group):
        other = ring(here, off, group)
        pl.semaphore_signal(
            barrier, inc=1,
            device_id={"section": sec, "dp": other // n_mp, "mp": lax.rem(other, n_mp)},
            device_id_type=MESH,
        )
    for off in range(1, n_sec):
        pl.semaphore_signal(
            barrier, inc=1,
            device_id={"section": ring(sec, off, n_sec), "dp": dp, "mp": mp},
            device_id_type=MESH,
        )

    def to(section, dp_at, mp_at, src, dst, send_sem, recv_sem):
        return pltpu.make_async_remote_copy(
            src_ref=src, dst_ref=dst, send_sem=send_sem, recv_sem=recv_sem,
            device_id={"section": section, "dp": dp_at, "mp": mp_at}, device_id_type=MESH,
        )

    def q_copy(off):
        return to(sec, ring(dp, off, n_dp), mp, queries, q_all.at[dp],
                  q_send.at[off], q_recv.at[off])

    def g_target(sub):
        column = mp * piece + sub * unit
        return column // w_cols, lax.rem(column, w_cols) // unit

    def g_source(at):
        return (dp * w_cols + at * unit) // piece

    def g_spot(chunk, source_dp, at):
        return g_all.at[
            chunk, pl.ds(pl.multiple_of(source_dp * CHUNK, CHUNK), CHUNK),
            pl.ds(pl.multiple_of(at * unit, unit), unit),
        ]

    def g_copy(chunk, sub, off):
        rows = pl.ds(pl.multiple_of(chunk * CHUNK, CHUNK), CHUNK)
        target, at = g_target(sub)
        return to(sec, target, ring(mp, off, n_mp), g_own.at[rows, sub * unit:(sub + 1) * unit],
                  g_spot(chunk, dp, at), g_send.at[chunk, sub, off], g_recv.at[chunk, at, dp])

    def g_move(chunk, act):
        for sub in range(piece // unit):
            target, _ = g_target(sub)
            for off in range(1, n_mp):
                act(g_copy(chunk, sub, off))

            @pl.when(target != dp)
            def _():
                act(g_copy(chunk, sub, 0))

    def g_send_all(chunk):
        g_move(chunk, lambda copy: copy.start())
        rows = pl.ds(pl.multiple_of(chunk * CHUNK, CHUNK), CHUNK)
        for sub in range(piece // unit):
            target, at = g_target(sub)

            @pl.when(target == dp)
            def _():
                g_spot(chunk, dp, at)[...] = g_own[rows, sub * unit:(sub + 1) * unit]

    def g_arrival(chunk, source_dp, at):
        spot = g_spot(chunk, source_dp, at)
        return to(sec, dp, mp, spot, spot, g_send.at[chunk, 0, 0], g_recv.at[chunk, at, source_dp])

    def g_wait(chunk):
        for at in range(w_cols // unit):
            source = g_source(at)
            for off in range(n_dp):
                source_dp = ring(dp, off, n_dp)
                arrival = g_arrival(chunk, source_dp, at)
                if off:
                    arrival.wait_recv()
                else:
                    pl.when(source != mp)(arrival.wait_recv)

    def s_copy(chunk, off):
        target = ring(dp, off, n_dp)
        return to(sec, target, mp,
                  sums_out.at[chunk, pl.ds(pl.multiple_of(target * CHUNK, CHUNK), CHUNK)],
                  sums_in.at[chunk, off], s_send.at[chunk, off], s_recv.at[chunk, off])

    def d_copy(chunk):
        rows = pl.ds(pl.multiple_of(chunk * CHUNK, CHUNK), CHUNK)
        return to(lax.rem(sec + n_sec - 1, n_sec), dp, mp, d_out.at[rows], d_in.at[rows],
                  d_send.at[chunk], d_recv.at[chunk])

    def in_copy(off):
        return to(sec, dp, ring(mp, off, n_mp), in_slots.at[0], in_slots.at[off],
                  in_send.at[off], in_recv.at[off])

    def out_copy(example, off):
        return to(sec, dp, ring(mp, off, n_mp), out_slots.at[0, example], out_slots.at[off, example],
                  out_send.at[example, off], out_recv.at[example, off])

    def a_copy():
        return to(0, dp, mp, total, layer_slots.at[sec], a_send, a_recv.at[sec])

    def b_copy(off):
        other = ring(here, off, group)
        return to(sec, other // n_mp, lax.rem(other, n_mp), section_slots.at[here],
                  section_slots.at[here], b_send.at[off], b_recv.at[off])

    def c_copy(section):
        return to(section, dp, mp, result, result, c_send.at[section], c_recv)

    load_pre.wait()
    slope_pre = pre[...].astype(jnp.float32)
    sigma = 1.0 / (1.0 + jnp.exp(-slope_pre))
    slope[...] = sigma * (1.0 + slope_pre * (1.0 - sigma))
    load_cot.wait()

    @pl.when(sec == top)
    def _():
        d_in[...] = cot[...]
        g_own[...] = (cot[...].astype(jnp.float32) * slope[...]).astype(jnp.bfloat16)

    pl.semaphore_wait(barrier, group - 1 + n_sec - 1)

    q_row = lax.broadcasted_iota(jnp.int32, total.shape, 0)
    r_lane = lax.broadcasted_iota(jnp.int32, total.shape, 1)

    def prepare():
        load_queries.wait()
        q_all[dp] = queries[...]
        for off in range(1, n_dp):
            q_copy(off).start()

        load_inputs.wait()
        load_in.wait()
        in_slots[0] = pack(dot_t(inputs[...], proj_in[...]))
        for off in range(1, n_mp):
            in_copy(off).start()

        spread = spread_out.shape
        spread_row = lax.broadcasted_iota(jnp.int32, spread, 0)
        spread_col = lax.broadcasted_iota(jnp.int32, spread, 1)
        spread_out[...] = (spread_row == spread_col % rank).astype(jnp.bfloat16)
        spread_in = (
            spread_row[:rank] == mp * piece_rank + spread_col[:rank] // rank
        ).astype(jnp.bfloat16)

        chosen = jnp.zeros(total.shape, jnp.float32)
        for round_at in range(rounds):
            for index in range(n_dp):
                spot = jnp.logical_and(q_row // asked == index, r_lane // examples == round_at)
                hit = jnp.where(partners[round_at, index] == dp, 1.0, 0.0).astype(jnp.float32)
                chosen = chosen + jnp.where(spot, hit, 0.0)
        mask[...] = chosen * (1.0 / (rank * math.sqrt(n_sec)))
        total[...] = jnp.zeros_like(total)

        q_pad[...] = jnp.zeros_like(q_pad)
        for off in range(1, n_dp):
            q_copy(off).wait_recv()
        for index in range(n_dp):
            q_pad[index * asked:(index + 1) * asked, :] = q_all[index]

        for off in range(1, n_mp):
            in_copy(off).wait_recv()
        in_side = in_slots[0]
        for off in range(1, n_mp):
            in_side = in_side + in_slots[off]
        in_side = unpack(in_side) * (1.0 / math.sqrt(LEN))
        in_high = in_side.astype(jnp.bfloat16)
        in_low = (in_side - in_high.astype(jnp.float32)).astype(jnp.bfloat16)
        in_wide[...] = (
            jnp.dot(in_high, spread_in, preferred_element_type=jnp.float32)
            + jnp.dot(in_low, spread_in, preferred_element_type=jnp.float32)
        )

    def step_rows(chunk):
        return pl.ds(pl.multiple_of(chunk * CHUNK, CHUNK), CHUNK)

    def take(chunk):
        rows = step_rows(chunk)
        d_copy(chunk).wait_recv()
        g_own[rows, :] = (d_in[rows, :].astype(jnp.float32) * slope[rows, :]).astype(jnp.bfloat16)

    def multiply(chunk):
        rows = step_rows(chunk)
        g_wait(chunk)
        for part in range(W_PARTS):
            cols = slice(part * w_rows, (part + 1) * w_rows)
            sums_out[chunk, :, cols] = dot_t(w_here[cols, :], g_all[chunk]).T
        for off in range(1, n_dp):
            s_copy(chunk, off).start()
        back = sums_out[chunk, pl.ds(pl.multiple_of(dp * CHUNK, CHUNK), CHUNK), :]
        for off in range(1, n_dp):
            s_copy(chunk, off).wait_recv()
            back = back + sums_in[chunk, off]
        d_out[rows, :] = (d_in[rows, :].astype(jnp.float32) + back).astype(jnp.bfloat16)
        d_copy(chunk).start()

    def project(example):
        rows = pl.ds(pl.multiple_of(example * LEN, LEN), LEN)
        out_slots[0, example] = dot_t(g_own[rows, :], proj_wide[...]).astype(jnp.bfloat16)
        for off in range(1, n_mp):
            out_copy(example, off).start()

    per = LEN // CHUNK

    def panel(example):
        out_side = jnp.zeros((LEN, out_slots.shape[3]), jnp.float32)
        for off in range(n_mp):
            if off:
                out_copy(example, off).wait_recv()
            out_side = out_side + out_slots[off, example].astype(jnp.float32)
        out_wide = jnp.dot(
            out_side.astype(jnp.bfloat16), spread_out[...], preferred_element_type=jnp.float32
        )
        rows = pl.ds(pl.multiple_of(example * LEN, LEN), LEN)
        row = jnp.sum(in_wide[rows, :] * out_wide, axis=0, keepdims=True)
        panels[0, pl.ds(example, 1), :] = row
        column = jnp.sum(q_pad[...] * row, axis=1, keepdims=True)
        total[...] += jnp.where(lax.rem(r_lane, examples) == example, column, 0.0)

    proj_wide[rank:, :] = jnp.zeros((proj_wide.shape[0] - rank, piece), jnp.bfloat16)
    load_out.wait()
    pl.when(sec < top)(prepare)
    load_w.wait()

    @pl.when(sec > 0)
    def _():
        @pl.loop(0, chunks + 1)
        def _(step):
            @pl.when(step < chunks)
            def _():
                @pl.when(sec < top)
                def _():
                    take(step)

                g_send_all(step)

            @pl.when(step > 0)
            def _():
                multiply(step - 1)

                @pl.when(lax.rem(step, per) == 0)
                def _():
                    project(step // per - 1)

        pl.when(sec == top)(prepare)

        @pl.loop(0, examples)
        def _(example):
            panel(example)

    @pl.when(sec == 0)
    def _():
        @pl.loop(0, chunks)
        def _(step):
            take(step)

            @pl.when(lax.rem(step, per) == per - 1)
            def _():
                project(step // per)

                @pl.when(step >= per)
                def _():
                    panel(step // per - 1)

        panel(examples - 1)

    share = total[...] * mask[...]

    @pl.when(sec > 0)
    def _():
        total[...] = share
        copy = a_copy()
        copy.start()
        copy.wait_send()
        c_copy(sec).wait_recv()

    @pl.when(sec == 0)
    def _():
        summed = share
        for section in range(1, n_sec):
            to(0, dp, mp, total, layer_slots.at[section], a_send, a_recv.at[section]).wait_recv()
            summed = summed + layer_slots[section]
        section_slots[here] = summed
        for off in range(1, group):
            b_copy(off).start()
        for off in range(1, group):
            b_copy(off).wait_recv()
        all_parts = section_slots[0]
        for slot in range(1, group):
            all_parts = all_parts + section_slots[slot]
        result[...] = all_parts
        for section in range(1, n_sec):
            c_copy(section).start()
        for off in range(1, group):
            b_copy(off).wait_send()
        for section in range(1, n_sec):
            c_copy(section).wait_send()

    for query in range(n_dp * asked):
        for round_at in range(rounds):
            table[query, round_at:round_at + 1, :] = result[
                query:query + 1, round_at * examples:(round_at + 1) * examples
            ]

    for off in range(1, n_dp):
        q_copy(off).wait_send()
    for off in range(1, n_mp):
        in_copy(off).wait_send()

    @pl.loop(0, examples)
    def _(example):
        for off in range(1, n_mp):
            out_copy(example, off).wait_send()

    @pl.when(sec > 0)
    def _():
        @pl.loop(0, chunks)
        def _(chunk):
            g_move(chunk, lambda copy: copy.wait_send())
            for off in range(1, n_dp):
                s_copy(chunk, off).wait_send()
            d_copy(chunk).wait_send()


def body(sizes, cotangent, saved_inputs, pre_acts, weights, proj_in, proj_out, query_panels, partners):
    n_sec, n_dp, n_mp = sizes
    tokens, piece = cotangent.shape
    width = piece * n_mp
    w_cols = weights.shape[2]
    unit = min(piece, w_cols)
    rank = proj_in.shape[2]
    examples = tokens // LEN
    asked = query_panels.shape[1]
    rounds = partners.shape[0]
    chunks = tokens // CHUNK
    panel = query_panels.shape[2]
    q_rows = -(-(n_dp * asked) // 8) * 8
    lanes = 128
    group = n_dp * n_mp
    dma = pltpu.SemaphoreType.DMA
    vmem = pl.BlockSpec(memory_space=pltpu.VMEM)
    hbm = pl.BlockSpec(memory_space=pltpu.HBM)
    return pl.pallas_call(
        functools.partial(relay_kernel, sizes),
        out_shape=(
            jax.ShapeDtypeStruct((1, examples, panel), jnp.float32),
            jax.ShapeDtypeStruct((n_dp * asked, rounds, examples), jnp.float32),
        ),
        in_specs=[hbm] * 7 + [pl.BlockSpec(memory_space=pltpu.SMEM)],
        out_specs=(vmem, vmem),
        scratch_shapes=[
            pltpu.VMEM((tokens, piece), jnp.bfloat16),
            pltpu.VMEM((tokens, piece), jnp.bfloat16),
            pltpu.VMEM((tokens, piece), jnp.bfloat16),
            pltpu.VMEM((piece, w_cols), jnp.bfloat16),
            pltpu.VMEM((rank, piece), jnp.bfloat16),
            pltpu.VMEM((2 * rank, piece), jnp.bfloat16),
            pltpu.VMEM((asked, panel), jnp.float32),
            pltpu.VMEM((tokens, piece), jnp.bfloat16),
            pltpu.VMEM((chunks, n_dp * CHUNK, w_cols), jnp.bfloat16),
            pltpu.VMEM((tokens, piece), jnp.bfloat16),
            pltpu.VMEM((tokens, piece), jnp.bfloat16),
            pltpu.VMEM((chunks, n_dp * CHUNK, piece), jnp.float32),
            pltpu.VMEM((chunks, n_dp, CHUNK, piece), jnp.float32),
            pltpu.VMEM((tokens, piece), jnp.float32),
            pltpu.VMEM((n_mp, tokens // 2, 2 * rank), jnp.float32),
            pltpu.VMEM((n_mp, examples, LEN, 2 * rank), jnp.bfloat16),
            pltpu.VMEM((tokens, panel), jnp.float32),
            pltpu.VMEM((n_dp, asked, panel), jnp.float32),
            pltpu.VMEM((q_rows, panel), jnp.float32),
            pltpu.VMEM((2 * rank, panel), jnp.bfloat16),
            pltpu.VMEM((q_rows, lanes), jnp.float32),
            pltpu.VMEM((n_sec, q_rows, lanes), jnp.float32),
            pltpu.VMEM((group, q_rows, lanes), jnp.float32),
            pltpu.VMEM((q_rows, lanes), jnp.float32),
            pltpu.VMEM((q_rows, lanes), jnp.float32),
            dma((7,)),
            dma((n_dp,)), dma((n_dp,)),
            dma((chunks, piece // unit, n_mp)), dma((chunks, w_cols // unit, n_dp)),
            dma((chunks,)), dma((chunks,)),
            dma((chunks, n_dp)), dma((chunks, n_dp)),
            dma((n_mp,)), dma((n_mp,)),
            dma((examples, n_mp)), dma((examples, n_mp)),
            dma, dma((n_sec,)),
            dma((group,)), dma((group,)),
            dma((n_sec,)), dma,
        ],
        compiler_params=pltpu.CompilerParams(
            collective_id=0, has_side_effects=True, vmem_limit_bytes=64 * 1024 * 1024
        ),
        cost_estimate=pl.CostEstimate(
            flops=2 * tokens * piece * width, bytes_accessed=2 * piece * w_cols, transcendentals=0
        ),
    )(cotangent, saved_inputs, pre_acts, weights, jnp.swapaxes(proj_in, 1, 2),
      jnp.swapaxes(proj_out, 1, 2), query_panels, partners)


def solution(mesh):
    placed = (
        P("dp", "mp"),
        P("section", "dp", "mp"),
        P("section", "dp", "mp"),
        P("section", "mp", "dp"),
        P("section", "mp", None),
        P("section", "mp", None),
        P("section", "dp", "mp"),
        P(),
    )
    sizes = (mesh.shape["section"], mesh.shape["dp"], mesh.shape["mp"])
    return jax.shard_map(
        functools.partial(body, sizes), mesh=mesh, in_specs=placed,
        out_specs=(P("section", "dp", "mp"), P()), check_vma=False,
    )
```

```python
import functools
import math

import jax
import jax.numpy as jnp
from jax import lax
from jax.experimental import pallas as pl
from jax.experimental.pallas import tpu as pltpu
from jax.sharding import PartitionSpec as P

LEN = 32
CHUNK = 16
W_PARTS = 4
MESH = pl.DeviceIdType.MESH


def ring(index, offset, count):
    return lax.rem(index + offset, count)


def dot_t(left, right):
    return lax.dot_general(
        left, right, (((1,), (1,)), ((), ())), preferred_element_type=jnp.float32
    )


def pack(block):
    half = block.shape[0] // 2
    return jnp.concatenate([block[:half], block[half:]], axis=1)


def unpack(block):
    half = block.shape[1] // 2
    return jnp.concatenate([block[:, :half], block[:, half:]], axis=0)


def relay_kernel(
    sizes, cot_hbm, inputs_hbm, pre_hbm, weights, proj_in_hbm, proj_out_hbm, queries_hbm, partners,
    panels, table,
    cot, inputs, pre, w_here, proj_in, proj_wide, queries,
    g_own, g_all, d_own, d_in, d_out, slope, in_slots, out_slots, in_wide, q_all, q_pad, spread_out, mask,
    layer_slots, section_slots, total, result,
    load, q_send, q_recv, g_send, g_recv, d_send, d_recv,
    in_send, in_recv, out_send, out_recv, a_send, a_recv, b_send, b_recv, c_send, c_recv,
):
    n_sec, n_dp, n_mp = sizes
    sec = lax.axis_index("section")
    dp = lax.axis_index("dp")
    mp = lax.axis_index("mp")
    tokens, piece = cot.shape
    loads = [
        pltpu.make_async_copy(src, dst, load.at[at])
        for at, (src, dst) in enumerate((
            (pre_hbm.at[0], pre), (cot_hbm, cot), (inputs_hbm.at[0], inputs),
            (proj_in_hbm.at[0], proj_in), (queries_hbm.at[0], queries),
            (proj_out_hbm.at[0], proj_wide.at[pl.ds(0, proj_out_hbm.shape[1])]), (weights.at[0], w_here),
        ))
    ]
    for copy in loads:
        copy.start()
    load_pre, load_cot, load_inputs, load_in, load_queries, load_out, load_w = loads
    chunks = tokens // CHUNK
    rank = proj_in.shape[0]
    examples = tokens // LEN
    piece_rank = rank // n_mp
    asked = queries.shape[0]
    rounds = partners.shape[0]
    w_cols = w_here.shape[1]
    w_rows = w_here.shape[0] // W_PARTS
    unit = min(piece, w_cols)
    top = n_sec - 1
    group = n_dp * n_mp
    here = dp * n_mp + mp

    barrier = pltpu.get_barrier_semaphore()
    for off in range(1, group):
        other = ring(here, off, group)
        pl.semaphore_signal(
            barrier, inc=1,
            device_id={"section": sec, "dp": other // n_mp, "mp": lax.rem(other, n_mp)},
            device_id_type=MESH,
        )
    for off in range(1, n_sec):
        pl.semaphore_signal(
            barrier, inc=1,
            device_id={"section": ring(sec, off, n_sec), "dp": dp, "mp": mp},
            device_id_type=MESH,
        )
    for step in (1, n_sec - 1):
        for off in range(1, n_dp):
            pl.semaphore_signal(
                barrier, inc=1,
                device_id={
                    "section": ring(sec, step, n_sec), "dp": ring(dp, off, n_dp), "mp": mp
                },
                device_id_type=MESH,
            )

    def to(section, dp_at, mp_at, src, dst, send_sem, recv_sem):
        return pltpu.make_async_remote_copy(
            src_ref=src, dst_ref=dst, send_sem=send_sem, recv_sem=recv_sem,
            device_id={"section": section, "dp": dp_at, "mp": mp_at}, device_id_type=MESH,
        )

    def q_copy(off):
        return to(sec, ring(dp, off, n_dp), mp, queries, q_all.at[dp],
                  q_send.at[off], q_recv.at[off])

    def g_target(sub):
        column = mp * piece + sub * unit
        return column // w_cols, lax.rem(column, w_cols) // unit

    def g_source(at):
        return (dp * w_cols + at * unit) // piece

    def g_spot(chunk, source_dp, at):
        return g_all.at[
            chunk, pl.ds(pl.multiple_of(source_dp * CHUNK, CHUNK), CHUNK),
            pl.ds(pl.multiple_of(at * unit, unit), unit),
        ]

    def g_copy(chunk, sub, off):
        rows = pl.ds(pl.multiple_of(chunk * CHUNK, CHUNK), CHUNK)
        target, at = g_target(sub)
        return to(sec, target, ring(mp, off, n_mp), g_own.at[rows, sub * unit:(sub + 1) * unit],
                  g_spot(chunk, dp, at), g_send.at[chunk, sub, off], g_recv.at[chunk, at, dp])

    def g_move(chunk, act):
        for sub in range(piece // unit):
            target, _ = g_target(sub)
            for off in range(1, n_mp):
                act(g_copy(chunk, sub, off))

            @pl.when(target != dp)
            def _():
                act(g_copy(chunk, sub, 0))

    def g_send_all(chunk):
        g_move(chunk, lambda copy: copy.start())
        rows = pl.ds(pl.multiple_of(chunk * CHUNK, CHUNK), CHUNK)
        for sub in range(piece // unit):
            target, at = g_target(sub)

            @pl.when(target == dp)
            def _():
                g_spot(chunk, dp, at)[...] = g_own[rows, sub * unit:(sub + 1) * unit]

    def g_arrival(chunk, source_dp, at):
        spot = g_spot(chunk, source_dp, at)
        return to(sec, dp, mp, spot, spot, g_send.at[chunk, 0, 0], g_recv.at[chunk, at, source_dp])

    def g_wait(chunk):
        for at in range(w_cols // unit):
            source = g_source(at)
            for off in range(n_dp):
                source_dp = ring(dp, off, n_dp)
                arrival = g_arrival(chunk, source_dp, at)
                if off:
                    arrival.wait_recv()
                else:
                    pl.when(source != mp)(arrival.wait_recv)

    def d_copy(chunk, target):
        rows = pl.ds(pl.multiple_of(chunk * CHUNK, CHUNK), CHUNK)
        return to(ring(sec, n_sec - 1, n_sec), target, mp,
                  d_out.at[chunk, target * CHUNK:(target + 1) * CHUNK], d_in.at[dp, rows],
                  d_send.at[chunk, target], d_recv.at[chunk, dp])

    def d_arrival(chunk, source):
        rows = pl.ds(pl.multiple_of(chunk * CHUNK, CHUNK), CHUNK)
        spot = d_in.at[source, rows]
        return to(sec, dp, mp, spot, spot, d_send.at[chunk, 0], d_recv.at[chunk, source])

    def in_copy(off):
        return to(sec, dp, ring(mp, off, n_mp), in_slots.at[0], in_slots.at[off],
                  in_send.at[off], in_recv.at[off])

    def out_copy(example, off):
        return to(sec, dp, ring(mp, off, n_mp), out_slots.at[0, example], out_slots.at[off, example],
                  out_send.at[example, off], out_recv.at[example, off])

    def a_copy():
        return to(0, dp, mp, total, layer_slots.at[sec], a_send, a_recv.at[sec])

    def b_copy(off):
        other = ring(here, off, group)
        return to(sec, other // n_mp, lax.rem(other, n_mp), section_slots.at[here],
                  section_slots.at[here], b_send.at[off], b_recv.at[off])

    def c_copy(section):
        return to(section, dp, mp, result, result, c_send.at[section], c_recv)

    load_pre.wait()
    slope_pre = pre[...].astype(jnp.float32)
    sigma = 1.0 / (1.0 + jnp.exp(-slope_pre))
    slope[...] = sigma * (1.0 + slope_pre * (1.0 - sigma))
    load_cot.wait()

    @pl.when(sec == top)
    def _():
        d_own[...] = cot[...]
        g_own[...] = (cot[...].astype(jnp.float32) * slope[...]).astype(jnp.bfloat16)

    pl.semaphore_wait(barrier, group - 1 + n_sec - 1 + 2 * (n_dp - 1))

    q_row = lax.broadcasted_iota(jnp.int32, total.shape, 0)
    r_lane = lax.broadcasted_iota(jnp.int32, total.shape, 1)

    def prepare():
        load_queries.wait()
        q_all[dp] = queries[...]
        for off in range(1, n_dp):
            q_copy(off).start()

        load_inputs.wait()
        load_in.wait()
        in_slots[0] = pack(dot_t(inputs[...], proj_in[...]))
        for off in range(1, n_mp):
            in_copy(off).start()

        spread = spread_out.shape
        spread_row = lax.broadcasted_iota(jnp.int32, spread, 0)
        spread_col = lax.broadcasted_iota(jnp.int32, spread, 1)
        spread_out[...] = (spread_row == spread_col % rank).astype(jnp.bfloat16)
        spread_in = (
            spread_row[:rank] == mp * piece_rank + spread_col[:rank] // rank
        ).astype(jnp.bfloat16)

        chosen = jnp.zeros(total.shape, jnp.float32)
        for round_at in range(rounds):
            for index in range(n_dp):
                spot = jnp.logical_and(q_row // asked == index, r_lane // examples == round_at)
                hit = jnp.where(partners[round_at, index] == dp, 1.0, 0.0).astype(jnp.float32)
                chosen = chosen + jnp.where(spot, hit, 0.0)
        mask[...] = chosen * (1.0 / (rank * math.sqrt(n_sec)))
        total[...] = jnp.zeros_like(total)

        q_pad[...] = jnp.zeros_like(q_pad)
        for off in range(1, n_dp):
            q_copy(off).wait_recv()
        for index in range(n_dp):
            q_pad[index * asked:(index + 1) * asked, :] = q_all[index]

        for off in range(1, n_mp):
            in_copy(off).wait_recv()
        in_side = in_slots[0]
        for off in range(1, n_mp):
            in_side = in_side + in_slots[off]
        in_side = unpack(in_side) * (1.0 / math.sqrt(LEN))
        in_high = in_side.astype(jnp.bfloat16)
        in_low = (in_side - in_high.astype(jnp.float32)).astype(jnp.bfloat16)
        in_wide[...] = (
            jnp.dot(in_high, spread_in, preferred_element_type=jnp.float32)
            + jnp.dot(in_low, spread_in, preferred_element_type=jnp.float32)
        )

    def step_rows(chunk):
        return pl.ds(pl.multiple_of(chunk * CHUNK, CHUNK), CHUNK)

    def take(chunk):
        rows = step_rows(chunk)
        delta = jnp.zeros((CHUNK, piece), jnp.float32)
        for source in range(n_dp):
            d_arrival(chunk, source).wait_recv()
            delta = delta + d_in[source, rows, :].astype(jnp.float32)
        delta = delta.astype(jnp.bfloat16)
        d_own[rows, :] = delta
        g_own[rows, :] = (delta.astype(jnp.float32) * slope[rows, :]).astype(jnp.bfloat16)

    def multiply(chunk):
        rows = step_rows(chunk)
        g_wait(chunk)
        for part in range(W_PARTS):
            cols = slice(part * w_rows, (part + 1) * w_rows)
            back = dot_t(w_here[cols, :], g_all[chunk]).T
            delta = d_own[rows, cols].astype(jnp.float32)
            for target in range(n_dp):
                at = slice(target * CHUNK, (target + 1) * CHUNK)
                d_out[chunk, at, cols] = (
                    back[at] + jnp.where(dp == target, delta, 0.0)
                ).astype(jnp.bfloat16)
        for target in range(n_dp):
            d_copy(chunk, target).start()

    def project(example):
        rows = pl.ds(pl.multiple_of(example * LEN, LEN), LEN)
        out_slots[0, example] = dot_t(g_own[rows, :], proj_wide[...]).astype(jnp.bfloat16)
        for off in range(1, n_mp):
            out_copy(example, off).start()

    per = LEN // CHUNK

    def panel(example):
        out_side = jnp.zeros((LEN, out_slots.shape[3]), jnp.float32)
        for off in range(n_mp):
            if off:
                out_copy(example, off).wait_recv()
            out_side = out_side + out_slots[off, example].astype(jnp.float32)
        out_wide = jnp.dot(
            out_side.astype(jnp.bfloat16), spread_out[...], preferred_element_type=jnp.float32
        )
        rows = pl.ds(pl.multiple_of(example * LEN, LEN), LEN)
        row = jnp.sum(in_wide[rows, :] * out_wide, axis=0, keepdims=True)
        panels[0, pl.ds(example, 1), :] = row
        column = jnp.sum(q_pad[...] * row, axis=1, keepdims=True)
        total[...] += jnp.where(lax.rem(r_lane, examples) == example, column, 0.0)

    proj_wide[rank:, :] = jnp.zeros((proj_wide.shape[0] - rank, piece), jnp.bfloat16)
    load_out.wait()
    pl.when(sec < top)(prepare)
    load_w.wait()

    @pl.when(sec > 0)
    def _():
        @pl.loop(0, chunks + 1)
        def _(step):
            @pl.when(step < chunks)
            def _():
                @pl.when(sec < top)
                def _():
                    take(step)

                g_send_all(step)

            @pl.when(step > 0)
            def _():
                multiply(step - 1)

                @pl.when(lax.rem(step, per) == 0)
                def _():
                    project(step // per - 1)

        pl.when(sec == top)(prepare)

        @pl.loop(0, examples)
        def _(example):
            panel(example)

    @pl.when(sec == 0)
    def _():
        @pl.loop(0, chunks)
        def _(step):
            take(step)

            @pl.when(lax.rem(step, per) == per - 1)
            def _():
                project(step // per)

                @pl.when(step >= per)
                def _():
                    panel(step // per - 1)

        panel(examples - 1)

    share = total[...] * mask[...]

    @pl.when(sec > 0)
    def _():
        total[...] = share
        copy = a_copy()
        copy.start()
        copy.wait_send()
        c_copy(sec).wait_recv()

    @pl.when(sec == 0)
    def _():
        summed = share
        for section in range(1, n_sec):
            to(0, dp, mp, total, layer_slots.at[section], a_send, a_recv.at[section]).wait_recv()
            summed = summed + layer_slots[section]
        section_slots[here] = summed
        for off in range(1, group):
            b_copy(off).start()
        for off in range(1, group):
            b_copy(off).wait_recv()
        all_parts = section_slots[0]
        for slot in range(1, group):
            all_parts = all_parts + section_slots[slot]
        result[...] = all_parts
        for section in range(1, n_sec):
            c_copy(section).start()
        for off in range(1, group):
            b_copy(off).wait_send()
        for section in range(1, n_sec):
            c_copy(section).wait_send()

    for query in range(n_dp * asked):
        for round_at in range(rounds):
            table[query, round_at:round_at + 1, :] = result[
                query:query + 1, round_at * examples:(round_at + 1) * examples
            ]

    for off in range(1, n_dp):
        q_copy(off).wait_send()
    for off in range(1, n_mp):
        in_copy(off).wait_send()

    @pl.loop(0, examples)
    def _(example):
        for off in range(1, n_mp):
            out_copy(example, off).wait_send()

    @pl.when(sec > 0)
    def _():
        @pl.loop(0, chunks)
        def _(chunk):
            g_move(chunk, lambda copy: copy.wait_send())
            for target in range(n_dp):
                d_copy(chunk, target).wait_send()


def body(sizes, cotangent, saved_inputs, pre_acts, weights, proj_in, proj_out, query_panels, partners):
    n_sec, n_dp, n_mp = sizes
    tokens, piece = cotangent.shape
    width = piece * n_mp
    w_cols = weights.shape[2]
    unit = min(piece, w_cols)
    rank = proj_in.shape[2]
    examples = tokens // LEN
    asked = query_panels.shape[1]
    rounds = partners.shape[0]
    chunks = tokens // CHUNK
    panel = query_panels.shape[2]
    q_rows = -(-(n_dp * asked) // 8) * 8
    lanes = 128
    group = n_dp * n_mp
    dma = pltpu.SemaphoreType.DMA
    vmem = pl.BlockSpec(memory_space=pltpu.VMEM)
    hbm = pl.BlockSpec(memory_space=pltpu.HBM)
    return pl.pallas_call(
        functools.partial(relay_kernel, sizes),
        out_shape=(
            jax.ShapeDtypeStruct((1, examples, panel), jnp.float32),
            jax.ShapeDtypeStruct((n_dp * asked, rounds, examples), jnp.float32),
        ),
        in_specs=[hbm] * 7 + [pl.BlockSpec(memory_space=pltpu.SMEM)],
        out_specs=(vmem, vmem),
        scratch_shapes=[
            pltpu.VMEM((tokens, piece), jnp.bfloat16),
            pltpu.VMEM((tokens, piece), jnp.bfloat16),
            pltpu.VMEM((tokens, piece), jnp.bfloat16),
            pltpu.VMEM((piece, w_cols), jnp.bfloat16),
            pltpu.VMEM((rank, piece), jnp.bfloat16),
            pltpu.VMEM((2 * rank, piece), jnp.bfloat16),
            pltpu.VMEM((asked, panel), jnp.float32),
            pltpu.VMEM((tokens, piece), jnp.bfloat16),
            pltpu.VMEM((chunks, n_dp * CHUNK, w_cols), jnp.bfloat16),
            pltpu.VMEM((tokens, piece), jnp.bfloat16),
            pltpu.VMEM((n_dp, tokens, piece), jnp.bfloat16),
            pltpu.VMEM((chunks, n_dp * CHUNK, piece), jnp.bfloat16),
            pltpu.VMEM((tokens, piece), jnp.float32),
            pltpu.VMEM((n_mp, tokens // 2, 2 * rank), jnp.float32),
            pltpu.VMEM((n_mp, examples, LEN, 2 * rank), jnp.bfloat16),
            pltpu.VMEM((tokens, panel), jnp.float32),
            pltpu.VMEM((n_dp, asked, panel), jnp.float32),
            pltpu.VMEM((q_rows, panel), jnp.float32),
            pltpu.VMEM((2 * rank, panel), jnp.bfloat16),
            pltpu.VMEM((q_rows, lanes), jnp.float32),
            pltpu.VMEM((n_sec, q_rows, lanes), jnp.float32),
            pltpu.VMEM((group, q_rows, lanes), jnp.float32),
            pltpu.VMEM((q_rows, lanes), jnp.float32),
            pltpu.VMEM((q_rows, lanes), jnp.float32),
            dma((7,)),
            dma((n_dp,)), dma((n_dp,)),
            dma((chunks, piece // unit, n_mp)), dma((chunks, w_cols // unit, n_dp)),
            dma((chunks, n_dp)), dma((chunks, n_dp)),
            dma((n_mp,)), dma((n_mp,)),
            dma((examples, n_mp)), dma((examples, n_mp)),
            dma, dma((n_sec,)),
            dma((group,)), dma((group,)),
            dma((n_sec,)), dma,
        ],
        compiler_params=pltpu.CompilerParams(
            collective_id=0, has_side_effects=True, vmem_limit_bytes=64 * 1024 * 1024
        ),
        cost_estimate=pl.CostEstimate(
            flops=2 * tokens * piece * width, bytes_accessed=2 * piece * w_cols, transcendentals=0
        ),
    )(cotangent, saved_inputs, pre_acts, weights, jnp.swapaxes(proj_in, 1, 2),
      jnp.swapaxes(proj_out, 1, 2), query_panels, partners)


def solution(mesh):
    placed = (
        P("dp", "mp"),
        P("section", "dp", "mp"),
        P("section", "dp", "mp"),
        P("section", "mp", "dp"),
        P("section", "mp", None),
        P("section", "mp", None),
        P("section", "dp", "mp"),
        P(),
    )
    sizes = (mesh.shape["section"], mesh.shape["dp"], mesh.shape["mp"])
    return jax.shard_map(
        functools.partial(body, sizes), mesh=mesh, in_specs=placed,
        out_specs=(P("section", "dp", "mp"), P()), check_vma=False,
    )
```

```python
import functools
import math

import jax
import jax.numpy as jnp
from jax import lax
from jax.experimental import pallas as pl
from jax.experimental.pallas import tpu as pltpu
from jax.sharding import PartitionSpec as P

LEN = 32
CHUNK = 16
W_PARTS = 4
MESH = pl.DeviceIdType.MESH


def ring(index, offset, count):
    return lax.rem(index + offset, count)


def dot_t(left, right):
    return lax.dot_general(
        left, right, (((1,), (1,)), ((), ())), preferred_element_type=jnp.float32
    )


def pack(block):
    half = block.shape[0] // 2
    return jnp.concatenate([block[:half], block[half:]], axis=1)


def unpack(block):
    half = block.shape[1] // 2
    return jnp.concatenate([block[:, :half], block[:, half:]], axis=0)


def relay_kernel(
    sizes, cot_hbm, inputs_hbm, pre_hbm, weights, proj_in_hbm, proj_out_hbm, queries_hbm, partners,
    panels, table,
    cot, inputs, pre, w_here, proj_in, proj_wide, queries,
    g_own, g_all, d_own, d_in, d_out, slope, in_slots, out_slots, in_wide, q_all, q_pad, spread_out, mask,
    layer_slots, section_slots, total, result,
    load, q_send, q_recv, g_send, g_recv, d_send, d_recv,
    in_send, in_recv, out_send, out_recv, a_send, a_recv, b_send, b_recv, c_send, c_recv,
):
    n_sec, n_dp, n_mp = sizes
    sec = lax.axis_index("section")
    dp = lax.axis_index("dp")
    mp = lax.axis_index("mp")
    tokens, piece = cot.shape
    loads = [
        pltpu.make_async_copy(src, dst, load.at[at])
        for at, (src, dst) in enumerate((
            (pre_hbm.at[0], pre), (cot_hbm, cot), (inputs_hbm.at[0], inputs),
            (proj_in_hbm.at[0], proj_in), (queries_hbm.at[0], queries),
            (proj_out_hbm.at[0], proj_wide.at[pl.ds(0, proj_out_hbm.shape[1])]), (weights.at[0], w_here),
        ))
    ]
    for copy in loads[:-1]:
        copy.start()
    load_pre, load_cot, load_inputs, load_in, load_queries, load_out, load_w = loads
    chunks = tokens // CHUNK
    rank = proj_in.shape[0]
    examples = tokens // LEN
    piece_rank = rank // n_mp
    asked = queries.shape[0]
    rounds = partners.shape[0]
    w_cols = w_here.shape[1]
    w_rows = w_here.shape[0] // W_PARTS
    unit = min(piece, w_cols)
    top = n_sec - 1
    group = n_dp * n_mp
    here = dp * n_mp + mp

    barrier = pltpu.get_barrier_semaphore()
    for off in range(1, group):
        other = ring(here, off, group)
        pl.semaphore_signal(
            barrier, inc=1,
            device_id={"section": sec, "dp": other // n_mp, "mp": lax.rem(other, n_mp)},
            device_id_type=MESH,
        )
    for off in range(1, n_sec):
        pl.semaphore_signal(
            barrier, inc=1,
            device_id={"section": ring(sec, off, n_sec), "dp": dp, "mp": mp},
            device_id_type=MESH,
        )
    for step in (1, n_sec - 1):
        for off in range(1, n_dp):
            pl.semaphore_signal(
                barrier, inc=1,
                device_id={
                    "section": ring(sec, step, n_sec), "dp": ring(dp, off, n_dp), "mp": mp
                },
                device_id_type=MESH,
            )

    def to(section, dp_at, mp_at, src, dst, send_sem, recv_sem):
        return pltpu.make_async_remote_copy(
            src_ref=src, dst_ref=dst, send_sem=send_sem, recv_sem=recv_sem,
            device_id={"section": section, "dp": dp_at, "mp": mp_at}, device_id_type=MESH,
        )

    def q_copy(off):
        return to(sec, ring(dp, off, n_dp), mp, queries, q_all.at[dp],
                  q_send.at[off], q_recv.at[off])

    def g_target(sub):
        column = mp * piece + sub * unit
        return column // w_cols, lax.rem(column, w_cols) // unit

    def g_source(at):
        return (dp * w_cols + at * unit) // piece

    def g_spot(chunk, source_dp, at):
        return g_all.at[
            chunk, pl.ds(pl.multiple_of(source_dp * CHUNK, CHUNK), CHUNK),
            pl.ds(pl.multiple_of(at * unit, unit), unit),
        ]

    def g_copy(chunk, sub, off):
        rows = pl.ds(pl.multiple_of(chunk * CHUNK, CHUNK), CHUNK)
        target, at = g_target(sub)
        return to(sec, target, ring(mp, off, n_mp), g_own.at[rows, sub * unit:(sub + 1) * unit],
                  g_spot(chunk, dp, at), g_send.at[chunk, sub, off], g_recv.at[chunk, at, dp])

    def g_move(chunk, act):
        for sub in range(piece // unit):
            target, _ = g_target(sub)
            for off in range(1, n_mp):
                act(g_copy(chunk, sub, off))

            @pl.when(target != dp)
            def _():
                act(g_copy(chunk, sub, 0))

    def g_send_all(chunk):
        g_move(chunk, lambda copy: copy.start())
        rows = pl.ds(pl.multiple_of(chunk * CHUNK, CHUNK), CHUNK)
        for sub in range(piece // unit):
            target, at = g_target(sub)

            @pl.when(target == dp)
            def _():
                g_spot(chunk, dp, at)[...] = g_own[rows, sub * unit:(sub + 1) * unit]

    def g_arrival(chunk, source_dp, at):
        spot = g_spot(chunk, source_dp, at)
        return to(sec, dp, mp, spot, spot, g_send.at[chunk, 0, 0], g_recv.at[chunk, at, source_dp])

    def g_wait(chunk):
        for at in range(w_cols // unit):
            source = g_source(at)
            for off in range(n_dp):
                source_dp = ring(dp, off, n_dp)
                arrival = g_arrival(chunk, source_dp, at)
                if off:
                    arrival.wait_recv()
                else:
                    pl.when(source != mp)(arrival.wait_recv)

    def d_copy(chunk, target):
        rows = pl.ds(pl.multiple_of(chunk * CHUNK, CHUNK), CHUNK)
        return to(ring(sec, n_sec - 1, n_sec), target, mp,
                  d_out.at[chunk, target * CHUNK:(target + 1) * CHUNK], d_in.at[dp, rows],
                  d_send.at[chunk, target], d_recv.at[chunk, dp])

    def d_arrival(chunk, source):
        rows = pl.ds(pl.multiple_of(chunk * CHUNK, CHUNK), CHUNK)
        spot = d_in.at[source, rows]
        return to(sec, dp, mp, spot, spot, d_send.at[chunk, 0], d_recv.at[chunk, source])

    def in_copy(off):
        return to(sec, dp, ring(mp, off, n_mp), in_slots.at[0], in_slots.at[off],
                  in_send.at[off], in_recv.at[off])

    def out_copy(example, off):
        return to(sec, dp, ring(mp, off, n_mp), out_slots.at[0, example], out_slots.at[off, example],
                  out_send.at[example, off], out_recv.at[example, off])

    def a_copy():
        return to(0, dp, mp, total, layer_slots.at[sec], a_send, a_recv.at[sec])

    def b_copy(off):
        other = ring(here, off, group)
        return to(sec, other // n_mp, lax.rem(other, n_mp), section_slots.at[here],
                  section_slots.at[here], b_send.at[off], b_recv.at[off])

    def c_copy(section):
        return to(section, dp, mp, result, result, c_send.at[section], c_recv)

    def set_slopes(rows):
        value = pre[rows, :].astype(jnp.float32)
        sigma = 1.0 / (1.0 + jnp.exp(-value))
        slope[rows, :] = sigma * (1.0 + value * (1.0 - sigma))

    load_pre.wait()
    load_cot.wait()
    load_w.start()
    pl.semaphore_wait(barrier, group - 1 + n_sec - 1 + 2 * (n_dp - 1))

    @pl.when(sec < top)
    def _():
        set_slopes(slice(0, tokens))

    q_row = lax.broadcasted_iota(jnp.int32, total.shape, 0)
    r_lane = lax.broadcasted_iota(jnp.int32, total.shape, 1)

    def prepare():
        load_queries.wait()
        q_all[dp] = queries[...]
        for off in range(1, n_dp):
            q_copy(off).start()

        load_inputs.wait()
        load_in.wait()
        in_slots[0] = pack(dot_t(inputs[...], proj_in[...]))
        for off in range(1, n_mp):
            in_copy(off).start()

        spread = spread_out.shape
        spread_row = lax.broadcasted_iota(jnp.int32, spread, 0)
        spread_col = lax.broadcasted_iota(jnp.int32, spread, 1)
        spread_out[...] = (spread_row == spread_col % rank).astype(jnp.bfloat16)
        spread_in = (
            spread_row[:rank] == mp * piece_rank + spread_col[:rank] // rank
        ).astype(jnp.bfloat16)

        chosen = jnp.zeros(total.shape, jnp.float32)
        for round_at in range(rounds):
            for index in range(n_dp):
                spot = jnp.logical_and(q_row // asked == index, r_lane // examples == round_at)
                hit = jnp.where(partners[round_at, index] == dp, 1.0, 0.0).astype(jnp.float32)
                chosen = chosen + jnp.where(spot, hit, 0.0)
        mask[...] = chosen * (1.0 / (rank * math.sqrt(n_sec)))
        total[...] = jnp.zeros_like(total)

        q_pad[...] = jnp.zeros_like(q_pad)
        for off in range(1, n_dp):
            q_copy(off).wait_recv()
        for index in range(n_dp):
            q_pad[index * asked:(index + 1) * asked, :] = q_all[index]

        for off in range(1, n_mp):
            in_copy(off).wait_recv()
        in_side = in_slots[0]
        for off in range(1, n_mp):
            in_side = in_side + in_slots[off]
        in_side = unpack(in_side) * (1.0 / math.sqrt(LEN))
        in_high = in_side.astype(jnp.bfloat16)
        in_low = (in_side - in_high.astype(jnp.float32)).astype(jnp.bfloat16)
        in_wide[...] = (
            jnp.dot(in_high, spread_in, preferred_element_type=jnp.float32)
            + jnp.dot(in_low, spread_in, preferred_element_type=jnp.float32)
        )

    def step_rows(chunk):
        return pl.ds(pl.multiple_of(chunk * CHUNK, CHUNK), CHUNK)

    def open_top(chunk):
        rows = step_rows(chunk)
        set_slopes(rows)
        d_own[rows, :] = cot[rows, :]
        g_own[rows, :] = (cot[rows, :].astype(jnp.float32) * slope[rows, :]).astype(jnp.bfloat16)

    def take(chunk):
        rows = step_rows(chunk)
        delta = jnp.zeros((CHUNK, piece), jnp.float32)
        for source in range(n_dp):
            d_arrival(chunk, source).wait_recv()
            delta = delta + d_in[source, rows, :].astype(jnp.float32)
        delta = delta.astype(jnp.bfloat16)
        d_own[rows, :] = delta
        g_own[rows, :] = (delta.astype(jnp.float32) * slope[rows, :]).astype(jnp.bfloat16)

    def multiply(chunk):
        rows = step_rows(chunk)
        g_wait(chunk)
        for part in range(W_PARTS):
            cols = slice(part * w_rows, (part + 1) * w_rows)
            back = dot_t(w_here[cols, :], g_all[chunk]).T
            delta = d_own[rows, cols].astype(jnp.float32)
            for target in range(n_dp):
                at = slice(target * CHUNK, (target + 1) * CHUNK)
                d_out[chunk, at, cols] = (
                    back[at] + jnp.where(dp == target, delta, 0.0)
                ).astype(jnp.bfloat16)
        for target in range(n_dp):
            d_copy(chunk, target).start()

    def project(example):
        rows = pl.ds(pl.multiple_of(example * LEN, LEN), LEN)
        out_slots[0, example] = dot_t(g_own[rows, :], proj_wide[...]).astype(jnp.bfloat16)
        for off in range(1, n_mp):
            out_copy(example, off).start()

    per = LEN // CHUNK

    def panel(example):
        out_side = jnp.zeros((LEN, out_slots.shape[3]), jnp.float32)
        for off in range(n_mp):
            if off:
                out_copy(example, off).wait_recv()
            out_side = out_side + out_slots[off, example].astype(jnp.float32)
        out_wide = jnp.dot(
            out_side.astype(jnp.bfloat16), spread_out[...], preferred_element_type=jnp.float32
        )
        rows = pl.ds(pl.multiple_of(example * LEN, LEN), LEN)
        row = jnp.sum(in_wide[rows, :] * out_wide, axis=0, keepdims=True)
        panels[0, pl.ds(example, 1), :] = row
        column = jnp.sum(q_pad[...] * row, axis=1, keepdims=True)
        total[...] += jnp.where(lax.rem(r_lane, examples) == example, column, 0.0)

    proj_wide[rank:, :] = jnp.zeros((proj_wide.shape[0] - rank, piece), jnp.bfloat16)
    load_out.wait()
    pl.when(sec < top)(prepare)

    @pl.when(sec > 0)
    def _():
        @pl.loop(0, chunks + 1)
        def _(step):
            pl.when(step == 1)(load_w.wait)

            @pl.when(step < chunks)
            def _():
                @pl.when(sec == top)
                def _():
                    open_top(step)

                @pl.when(sec < top)
                def _():
                    take(step)

                g_send_all(step)

            @pl.when(step > 0)
            def _():
                multiply(step - 1)

                @pl.when(lax.rem(step, per) == 0)
                def _():
                    project(step // per - 1)

        pl.when(sec == top)(prepare)

        @pl.loop(0, examples)
        def _(example):
            panel(example)

    @pl.when(sec == 0)
    def _():
        load_w.wait()

        @pl.loop(0, chunks)
        def _(step):
            take(step)

            @pl.when(lax.rem(step, per) == per - 1)
            def _():
                project(step // per)

                @pl.when(step >= per)
                def _():
                    panel(step // per - 1)

        panel(examples - 1)

    share = total[...] * mask[...]

    @pl.when(sec > 0)
    def _():
        total[...] = share
        copy = a_copy()
        copy.start()
        copy.wait_send()
        c_copy(sec).wait_recv()

    @pl.when(sec == 0)
    def _():
        summed = share
        for section in range(1, n_sec):
            to(0, dp, mp, total, layer_slots.at[section], a_send, a_recv.at[section]).wait_recv()
            summed = summed + layer_slots[section]
        section_slots[here] = summed
        for off in range(1, group):
            b_copy(off).start()
        for off in range(1, group):
            b_copy(off).wait_recv()
        all_parts = section_slots[0]
        for slot in range(1, group):
            all_parts = all_parts + section_slots[slot]
        result[...] = all_parts
        for section in range(1, n_sec):
            c_copy(section).start()
        for off in range(1, group):
            b_copy(off).wait_send()
        for section in range(1, n_sec):
            c_copy(section).wait_send()

    for query in range(n_dp * asked):
        for round_at in range(rounds):
            table[query, round_at:round_at + 1, :] = result[
                query:query + 1, round_at * examples:(round_at + 1) * examples
            ]

    for off in range(1, n_dp):
        q_copy(off).wait_send()
    for off in range(1, n_mp):
        in_copy(off).wait_send()

    @pl.loop(0, examples)
    def _(example):
        for off in range(1, n_mp):
            out_copy(example, off).wait_send()

    @pl.when(sec > 0)
    def _():
        @pl.loop(0, chunks)
        def _(chunk):
            g_move(chunk, lambda copy: copy.wait_send())
            for target in range(n_dp):
                d_copy(chunk, target).wait_send()


def hand_over_kernel(panels, table, panels_out, table_out, done):
    copies = [
        pltpu.make_async_copy(panels, panels_out, done.at[0]),
        pltpu.make_async_copy(table, table_out, done.at[1]),
    ]
    for copy in copies:
        copy.start()
    for copy in copies:
        copy.wait()


def body(sizes, cotangent, saved_inputs, pre_acts, weights, proj_in, proj_out, query_panels, partners):
    n_sec, n_dp, n_mp = sizes
    tokens, piece = cotangent.shape
    width = piece * n_mp
    w_cols = weights.shape[2]
    unit = min(piece, w_cols)
    rank = proj_in.shape[2]
    examples = tokens // LEN
    asked = query_panels.shape[1]
    rounds = partners.shape[0]
    chunks = tokens // CHUNK
    panel = query_panels.shape[2]
    q_rows = -(-(n_dp * asked) // 8) * 8
    lanes = 128
    group = n_dp * n_mp
    dma = pltpu.SemaphoreType.DMA
    vmem = pl.BlockSpec(memory_space=pltpu.VMEM)
    hbm = pl.BlockSpec(memory_space=pltpu.HBM)
    results = (
        jax.ShapeDtypeStruct((1, examples, panel), jnp.float32),
        jax.ShapeDtypeStruct((n_dp * asked, rounds, examples), jnp.float32),
    )
    made = pl.pallas_call(
        functools.partial(relay_kernel, sizes),
        out_shape=results,
        in_specs=[hbm] * 7 + [pl.BlockSpec(memory_space=pltpu.SMEM)],
        out_specs=(vmem, vmem),
        scratch_shapes=[
            pltpu.VMEM((tokens, piece), jnp.bfloat16),
            pltpu.VMEM((tokens, piece), jnp.bfloat16),
            pltpu.VMEM((tokens, piece), jnp.bfloat16),
            pltpu.VMEM((piece, w_cols), jnp.bfloat16),
            pltpu.VMEM((rank, piece), jnp.bfloat16),
            pltpu.VMEM((2 * rank, piece), jnp.bfloat16),
            pltpu.VMEM((asked, panel), jnp.float32),
            pltpu.VMEM((tokens, piece), jnp.bfloat16),
            pltpu.VMEM((chunks, n_dp * CHUNK, w_cols), jnp.bfloat16),
            pltpu.VMEM((tokens, piece), jnp.bfloat16),
            pltpu.VMEM((n_dp, tokens, piece), jnp.bfloat16),
            pltpu.VMEM((chunks, n_dp * CHUNK, piece), jnp.bfloat16),
            pltpu.VMEM((tokens, piece), jnp.float32),
            pltpu.VMEM((n_mp, tokens // 2, 2 * rank), jnp.float32),
            pltpu.VMEM((n_mp, examples, LEN, 2 * rank), jnp.bfloat16),
            pltpu.VMEM((tokens, panel), jnp.float32),
            pltpu.VMEM((n_dp, asked, panel), jnp.float32),
            pltpu.VMEM((q_rows, panel), jnp.float32),
            pltpu.VMEM((2 * rank, panel), jnp.bfloat16),
            pltpu.VMEM((q_rows, lanes), jnp.float32),
            pltpu.VMEM((n_sec, q_rows, lanes), jnp.float32),
            pltpu.VMEM((group, q_rows, lanes), jnp.float32),
            pltpu.VMEM((q_rows, lanes), jnp.float32),
            pltpu.VMEM((q_rows, lanes), jnp.float32),
            dma((7,)),
            dma((n_dp,)), dma((n_dp,)),
            dma((chunks, piece // unit, n_mp)), dma((chunks, w_cols // unit, n_dp)),
            dma((chunks, n_dp)), dma((chunks, n_dp)),
            dma((n_mp,)), dma((n_mp,)),
            dma((examples, n_mp)), dma((examples, n_mp)),
            dma, dma((n_sec,)),
            dma((group,)), dma((group,)),
            dma((n_sec,)), dma,
        ],
        compiler_params=pltpu.CompilerParams(
            collective_id=0, has_side_effects=True, vmem_limit_bytes=64 * 1024 * 1024
        ),
        cost_estimate=pl.CostEstimate(
            flops=2 * tokens * piece * width, bytes_accessed=2 * piece * w_cols, transcendentals=0
        ),
    )(cotangent, saved_inputs, pre_acts, weights, jnp.swapaxes(proj_in, 1, 2),
      jnp.swapaxes(proj_out, 1, 2), query_panels, partners)
    return pl.pallas_call(
        hand_over_kernel,
        out_shape=results,
        in_specs=[hbm, hbm],
        out_specs=(hbm, hbm),
        scratch_shapes=[dma((2,))],
        compiler_params=pltpu.CompilerParams(vmem_limit_bytes=64 * 1024 * 1024),
    )(*made)


def solution(mesh):
    placed = (
        P("dp", "mp"),
        P("section", "dp", "mp"),
        P("section", "dp", "mp"),
        P("section", "mp", "dp"),
        P("section", "mp", None),
        P("section", "mp", None),
        P("section", "dp", "mp"),
        P(),
    )
    sizes = (mesh.shape["section"], mesh.shape["dp"], mesh.shape["mp"])
    return jax.shard_map(
        functools.partial(body, sizes), mesh=mesh, in_specs=placed,
        out_specs=(P("section", "dp", "mp"), P()), check_vma=False,
    )
```

```python
import functools
import math

import jax
import jax.numpy as jnp
from jax import lax
from jax.experimental import pallas as pl
from jax.experimental.pallas import tpu as pltpu
from jax.sharding import PartitionSpec as P

LEN = 32
CHUNK = 16
W_PARTS = 4
D_PARTS = 2
MESH = pl.DeviceIdType.MESH


def ring(index, offset, count):
    return lax.rem(index + offset, count)


def dot_t(left, right):
    return lax.dot_general(
        left, right, (((1,), (1,)), ((), ())), preferred_element_type=jnp.float32
    )


def pack(block):
    half = block.shape[0] // 2
    return jnp.concatenate([block[:half], block[half:]], axis=1)


def unpack(block):
    half = block.shape[1] // 2
    return jnp.concatenate([block[:, :half], block[:, half:]], axis=0)


def relay_kernel(
    sizes, cot_hbm, inputs_hbm, pre_hbm, weights, proj_in_hbm, proj_out_hbm, queries_hbm, partners,
    panels, table,
    cot, inputs, pre, w_here, proj_in, proj_wide, queries,
    g_own, g_all, d_own, d_in, d_out, slope, in_slots, out_slots, in_wide, q_all, q_pad, spread_out, mask,
    layer_slots, section_slots, total, result,
    load, q_send, q_recv, g_send, g_recv, d_send, d_recv,
    in_send, in_recv, out_send, out_recv, a_send, a_recv, b_send, b_recv, c_send, c_recv,
):
    n_sec, n_dp, n_mp = sizes
    sec = lax.axis_index("section")
    dp = lax.axis_index("dp")
    mp = lax.axis_index("mp")
    tokens, piece = cot.shape
    loads = [
        pltpu.make_async_copy(src, dst, load.at[at])
        for at, (src, dst) in enumerate((
            (pre_hbm.at[0], pre), (cot_hbm, cot), (inputs_hbm.at[0], inputs),
            (proj_in_hbm.at[0], proj_in), (queries_hbm.at[0], queries),
            (proj_out_hbm.at[0], proj_wide.at[pl.ds(0, proj_out_hbm.shape[1])]), (weights.at[0], w_here),
        ))
    ]
    for copy in loads[:-1]:
        copy.start()
    load_pre, load_cot, load_inputs, load_in, load_queries, load_out, load_w = loads
    chunks = tokens // CHUNK
    rank = proj_in.shape[0]
    examples = tokens // LEN
    piece_rank = rank // n_mp
    asked = queries.shape[0]
    rounds = partners.shape[0]
    w_cols = w_here.shape[1]
    w_rows = w_here.shape[0] // W_PARTS
    unit = min(piece, w_cols)
    top = n_sec - 1
    group = n_dp * n_mp
    here = dp * n_mp + mp

    barrier = pltpu.get_barrier_semaphore()
    for off in range(1, group):
        other = ring(here, off, group)
        pl.semaphore_signal(
            barrier, inc=1,
            device_id={"section": sec, "dp": other // n_mp, "mp": lax.rem(other, n_mp)},
            device_id_type=MESH,
        )
    for off in range(1, n_sec):
        pl.semaphore_signal(
            barrier, inc=1,
            device_id={"section": ring(sec, off, n_sec), "dp": dp, "mp": mp},
            device_id_type=MESH,
        )
    for step in (1, n_sec - 1):
        for off in range(1, n_dp):
            pl.semaphore_signal(
                barrier, inc=1,
                device_id={
                    "section": ring(sec, step, n_sec), "dp": ring(dp, off, n_dp), "mp": mp
                },
                device_id_type=MESH,
            )

    def to(section, dp_at, mp_at, src, dst, send_sem, recv_sem):
        return pltpu.make_async_remote_copy(
            src_ref=src, dst_ref=dst, send_sem=send_sem, recv_sem=recv_sem,
            device_id={"section": section, "dp": dp_at, "mp": mp_at}, device_id_type=MESH,
        )

    def q_copy(off):
        return to(sec, ring(dp, off, n_dp), mp, queries, q_all.at[dp],
                  q_send.at[off], q_recv.at[off])

    def g_target(sub):
        column = mp * piece + sub * unit
        return column // w_cols, lax.rem(column, w_cols) // unit

    def g_source(at):
        return (dp * w_cols + at * unit) // piece

    def g_spot(chunk, source_dp, at):
        return g_all.at[
            chunk, pl.ds(pl.multiple_of(source_dp * CHUNK, CHUNK), CHUNK),
            pl.ds(pl.multiple_of(at * unit, unit), unit),
        ]

    def g_copy(chunk, sub, off):
        rows = pl.ds(pl.multiple_of(chunk * CHUNK, CHUNK), CHUNK)
        target, at = g_target(sub)
        return to(sec, target, ring(mp, off, n_mp), g_own.at[rows, sub * unit:(sub + 1) * unit],
                  g_spot(chunk, dp, at), g_send.at[chunk, sub, off], g_recv.at[chunk, at, dp])

    def g_move(chunk, act):
        for sub in range(piece // unit):
            target, _ = g_target(sub)
            for off in range(1, n_mp):
                act(g_copy(chunk, sub, off))

            @pl.when(target != dp)
            def _():
                act(g_copy(chunk, sub, 0))

    def g_send_all(chunk):
        g_move(chunk, lambda copy: copy.start())
        rows = pl.ds(pl.multiple_of(chunk * CHUNK, CHUNK), CHUNK)
        for sub in range(piece // unit):
            target, at = g_target(sub)

            @pl.when(target == dp)
            def _():
                g_spot(chunk, dp, at)[...] = g_own[rows, sub * unit:(sub + 1) * unit]

    def g_arrival(chunk, source_dp, at):
        spot = g_spot(chunk, source_dp, at)
        return to(sec, dp, mp, spot, spot, g_send.at[chunk, 0, 0], g_recv.at[chunk, at, source_dp])

    def g_wait(chunk):
        for at in range(w_cols // unit):
            source = g_source(at)
            for off in range(n_dp):
                source_dp = ring(dp, off, n_dp)
                arrival = g_arrival(chunk, source_dp, at)
                if off:
                    arrival.wait_recv()
                else:
                    pl.when(source != mp)(arrival.wait_recv)

    d_width = piece // D_PARTS

    def d_copy(chunk, part, target):
        rows = pl.ds(pl.multiple_of(chunk * CHUNK, CHUNK), CHUNK)
        cols = slice(part * d_width, (part + 1) * d_width)
        return to(ring(sec, n_sec - 1, n_sec), target, mp,
                  d_out.at[chunk, target * CHUNK:(target + 1) * CHUNK, cols],
                  d_in.at[dp, rows, cols],
                  d_send.at[chunk, part, target], d_recv.at[chunk, part, dp])

    def d_arrival(chunk, part, source):
        rows = pl.ds(pl.multiple_of(chunk * CHUNK, CHUNK), CHUNK)
        spot = d_in.at[source, rows, part * d_width:(part + 1) * d_width]
        return to(sec, dp, mp, spot, spot, d_send.at[chunk, part, 0],
                  d_recv.at[chunk, part, source])

    def in_copy(off):
        return to(sec, dp, ring(mp, off, n_mp), in_slots.at[0], in_slots.at[off],
                  in_send.at[off], in_recv.at[off])

    def out_copy(example, off):
        return to(sec, dp, ring(mp, off, n_mp), out_slots.at[0, example], out_slots.at[off, example],
                  out_send.at[example, off], out_recv.at[example, off])

    def a_copy():
        return to(0, dp, mp, total, layer_slots.at[sec], a_send, a_recv.at[sec])

    def b_copy(off):
        other = ring(here, off, group)
        return to(sec, other // n_mp, lax.rem(other, n_mp), section_slots.at[here],
                  section_slots.at[here], b_send.at[off], b_recv.at[off])

    def c_copy(section):
        return to(section, dp, mp, result, result, c_send.at[section], c_recv)

    def set_slopes(rows):
        value = pre[rows, :].astype(jnp.float32)
        sigma = 1.0 / (1.0 + jnp.exp(-value))
        slope[rows, :] = sigma * (1.0 + value * (1.0 - sigma))

    load_pre.wait()
    load_cot.wait()
    load_w.start()
    pl.semaphore_wait(barrier, group - 1 + n_sec - 1 + 2 * (n_dp - 1))

    @pl.when(sec < top)
    def _():
        set_slopes(slice(0, tokens))

    q_row = lax.broadcasted_iota(jnp.int32, total.shape, 0)
    r_lane = lax.broadcasted_iota(jnp.int32, total.shape, 1)

    def prepare():
        load_queries.wait()
        q_all[dp] = queries[...]
        for off in range(1, n_dp):
            q_copy(off).start()

        load_inputs.wait()
        load_in.wait()
        in_slots[0] = pack(dot_t(inputs[...], proj_in[...]))
        for off in range(1, n_mp):
            in_copy(off).start()

        spread = spread_out.shape
        spread_row = lax.broadcasted_iota(jnp.int32, spread, 0)
        spread_col = lax.broadcasted_iota(jnp.int32, spread, 1)
        spread_out[...] = (spread_row == spread_col % rank).astype(jnp.bfloat16)
        spread_in = (
            spread_row[:rank] == mp * piece_rank + spread_col[:rank] // rank
        ).astype(jnp.bfloat16)

        chosen = jnp.zeros(total.shape, jnp.float32)
        for round_at in range(rounds):
            for index in range(n_dp):
                spot = jnp.logical_and(q_row // asked == index, r_lane // examples == round_at)
                hit = jnp.where(partners[round_at, index] == dp, 1.0, 0.0).astype(jnp.float32)
                chosen = chosen + jnp.where(spot, hit, 0.0)
        mask[...] = chosen * (1.0 / (rank * math.sqrt(n_sec)))
        total[...] = jnp.zeros_like(total)

        q_pad[...] = jnp.zeros_like(q_pad)
        for off in range(1, n_dp):
            q_copy(off).wait_recv()
        for index in range(n_dp):
            q_pad[index * asked:(index + 1) * asked, :] = q_all[index]

        for off in range(1, n_mp):
            in_copy(off).wait_recv()
        in_side = in_slots[0]
        for off in range(1, n_mp):
            in_side = in_side + in_slots[off]
        in_side = unpack(in_side) * (1.0 / math.sqrt(LEN))
        in_high = in_side.astype(jnp.bfloat16)
        in_low = (in_side - in_high.astype(jnp.float32)).astype(jnp.bfloat16)
        in_wide[...] = (
            jnp.dot(in_high, spread_in, preferred_element_type=jnp.float32)
            + jnp.dot(in_low, spread_in, preferred_element_type=jnp.float32)
        )

    def step_rows(chunk):
        return pl.ds(pl.multiple_of(chunk * CHUNK, CHUNK), CHUNK)

    def open_top(chunk):
        rows = step_rows(chunk)
        set_slopes(rows)
        d_own[rows, :] = cot[rows, :]
        g_own[rows, :] = (cot[rows, :].astype(jnp.float32) * slope[rows, :]).astype(jnp.bfloat16)

    def take(chunk):
        rows = step_rows(chunk)
        for part in range(D_PARTS):
            cols = slice(part * d_width, (part + 1) * d_width)
            delta = jnp.zeros((CHUNK, d_width), jnp.float32)
            for source in range(n_dp):
                d_arrival(chunk, part, source).wait_recv()
                delta = delta + d_in[source, rows, cols].astype(jnp.float32)
            delta = delta.astype(jnp.bfloat16)
            d_own[rows, cols] = delta
            g_own[rows, cols] = (
                delta.astype(jnp.float32) * slope[rows, cols]
            ).astype(jnp.bfloat16)

    def multiply(chunk):
        rows = step_rows(chunk)
        g_wait(chunk)
        for part in range(W_PARTS):
            cols = slice(part * w_rows, (part + 1) * w_rows)
            back = dot_t(w_here[cols, :], g_all[chunk]).T
            delta = d_own[rows, cols].astype(jnp.float32)
            for target in range(n_dp):
                at = slice(target * CHUNK, (target + 1) * CHUNK)
                d_out[chunk, at, cols] = (
                    back[at] + jnp.where(dp == target, delta, 0.0)
                ).astype(jnp.bfloat16)
            if (part + 1) % (W_PARTS // D_PARTS) == 0:
                for target in range(n_dp):
                    d_copy(chunk, part // (W_PARTS // D_PARTS), target).start()

    def project(example):
        rows = pl.ds(pl.multiple_of(example * LEN, LEN), LEN)
        out_slots[0, example] = dot_t(g_own[rows, :], proj_wide[...]).astype(jnp.bfloat16)
        for off in range(1, n_mp):
            out_copy(example, off).start()

    per = LEN // CHUNK

    def panel(example):
        out_side = jnp.zeros((LEN, out_slots.shape[3]), jnp.float32)
        for off in range(n_mp):
            if off:
                out_copy(example, off).wait_recv()
            out_side = out_side + out_slots[off, example].astype(jnp.float32)
        out_wide = jnp.dot(
            out_side.astype(jnp.bfloat16), spread_out[...], preferred_element_type=jnp.float32
        )
        rows = pl.ds(pl.multiple_of(example * LEN, LEN), LEN)
        row = jnp.sum(in_wide[rows, :] * out_wide, axis=0, keepdims=True)
        panels[0, pl.ds(example, 1), :] = row
        column = jnp.sum(q_pad[...] * row, axis=1, keepdims=True)
        total[...] += jnp.where(lax.rem(r_lane, examples) == example, column, 0.0)

    proj_wide[rank:, :] = jnp.zeros((proj_wide.shape[0] - rank, piece), jnp.bfloat16)
    load_out.wait()
    pl.when(sec < top)(prepare)

    @pl.when(sec > 0)
    def _():
        @pl.loop(0, chunks + 1)
        def _(step):
            pl.when(step == 1)(load_w.wait)

            @pl.when(step < chunks)
            def _():
                @pl.when(sec == top)
                def _():
                    open_top(step)

                @pl.when(sec < top)
                def _():
                    take(step)

                g_send_all(step)

            @pl.when(step > 0)
            def _():
                multiply(step - 1)

                @pl.when(lax.rem(step, per) == 0)
                def _():
                    project(step // per - 1)

        pl.when(sec == top)(prepare)

        @pl.loop(0, examples)
        def _(example):
            panel(example)

    @pl.when(sec == 0)
    def _():
        load_w.wait()

        @pl.loop(0, chunks)
        def _(step):
            take(step)

            @pl.when(lax.rem(step, per) == per - 1)
            def _():
                project(step // per)

                @pl.when(step >= per)
                def _():
                    panel(step // per - 1)

        panel(examples - 1)

    share = total[...] * mask[...]

    @pl.when(sec > 0)
    def _():
        total[...] = share
        copy = a_copy()
        copy.start()
        copy.wait_send()
        c_copy(sec).wait_recv()

    @pl.when(sec == 0)
    def _():
        summed = share
        for section in range(1, n_sec):
            to(0, dp, mp, total, layer_slots.at[section], a_send, a_recv.at[section]).wait_recv()
            summed = summed + layer_slots[section]
        section_slots[here] = summed
        for off in range(1, group):
            b_copy(off).start()
        for off in range(1, group):
            b_copy(off).wait_recv()
        all_parts = section_slots[0]
        for slot in range(1, group):
            all_parts = all_parts + section_slots[slot]
        result[...] = all_parts
        for section in range(1, n_sec):
            c_copy(section).start()
        for off in range(1, group):
            b_copy(off).wait_send()
        for section in range(1, n_sec):
            c_copy(section).wait_send()

    for query in range(n_dp * asked):
        for round_at in range(rounds):
            table[query, round_at:round_at + 1, :] = result[
                query:query + 1, round_at * examples:(round_at + 1) * examples
            ]

    for off in range(1, n_dp):
        q_copy(off).wait_send()
    for off in range(1, n_mp):
        in_copy(off).wait_send()

    @pl.loop(0, examples)
    def _(example):
        for off in range(1, n_mp):
            out_copy(example, off).wait_send()

    @pl.when(sec > 0)
    def _():
        @pl.loop(0, chunks)
        def _(chunk):
            g_move(chunk, lambda copy: copy.wait_send())
            for part in range(D_PARTS):
                for target in range(n_dp):
                    d_copy(chunk, part, target).wait_send()


def hand_over_kernel(panels, table, panels_out, table_out, done):
    copies = [
        pltpu.make_async_copy(panels, panels_out, done.at[0]),
        pltpu.make_async_copy(table, table_out, done.at[1]),
    ]
    for copy in copies:
        copy.start()
    for copy in copies:
        copy.wait()


def body(sizes, cotangent, saved_inputs, pre_acts, weights, proj_in, proj_out, query_panels, partners):
    n_sec, n_dp, n_mp = sizes
    tokens, piece = cotangent.shape
    width = piece * n_mp
    w_cols = weights.shape[2]
    unit = min(piece, w_cols)
    rank = proj_in.shape[2]
    examples = tokens // LEN
    asked = query_panels.shape[1]
    rounds = partners.shape[0]
    chunks = tokens // CHUNK
    panel = query_panels.shape[2]
    q_rows = -(-(n_dp * asked) // 8) * 8
    lanes = 128
    group = n_dp * n_mp
    dma = pltpu.SemaphoreType.DMA
    vmem = pl.BlockSpec(memory_space=pltpu.VMEM)
    hbm = pl.BlockSpec(memory_space=pltpu.HBM)
    results = (
        jax.ShapeDtypeStruct((1, examples, panel), jnp.float32),
        jax.ShapeDtypeStruct((n_dp * asked, rounds, examples), jnp.float32),
    )
    made = pl.pallas_call(
        functools.partial(relay_kernel, sizes),
        out_shape=results,
        in_specs=[hbm] * 7 + [pl.BlockSpec(memory_space=pltpu.SMEM)],
        out_specs=(vmem, vmem),
        scratch_shapes=[
            pltpu.VMEM((tokens, piece), jnp.bfloat16),
            pltpu.VMEM((tokens, piece), jnp.bfloat16),
            pltpu.VMEM((tokens, piece), jnp.bfloat16),
            pltpu.VMEM((piece, w_cols), jnp.bfloat16),
            pltpu.VMEM((rank, piece), jnp.bfloat16),
            pltpu.VMEM((2 * rank, piece), jnp.bfloat16),
            pltpu.VMEM((asked, panel), jnp.float32),
            pltpu.VMEM((tokens, piece), jnp.bfloat16),
            pltpu.VMEM((chunks, n_dp * CHUNK, w_cols), jnp.bfloat16),
            pltpu.VMEM((tokens, piece), jnp.bfloat16),
            pltpu.VMEM((n_dp, tokens, piece), jnp.bfloat16),
            pltpu.VMEM((chunks, n_dp * CHUNK, piece), jnp.bfloat16),
            pltpu.VMEM((tokens, piece), jnp.float32),
            pltpu.VMEM((n_mp, tokens // 2, 2 * rank), jnp.float32),
            pltpu.VMEM((n_mp, examples, LEN, 2 * rank), jnp.bfloat16),
            pltpu.VMEM((tokens, panel), jnp.float32),
            pltpu.VMEM((n_dp, asked, panel), jnp.float32),
            pltpu.VMEM((q_rows, panel), jnp.float32),
            pltpu.VMEM((2 * rank, panel), jnp.bfloat16),
            pltpu.VMEM((q_rows, lanes), jnp.float32),
            pltpu.VMEM((n_sec, q_rows, lanes), jnp.float32),
            pltpu.VMEM((group, q_rows, lanes), jnp.float32),
            pltpu.VMEM((q_rows, lanes), jnp.float32),
            pltpu.VMEM((q_rows, lanes), jnp.float32),
            dma((7,)),
            dma((n_dp,)), dma((n_dp,)),
            dma((chunks, piece // unit, n_mp)), dma((chunks, w_cols // unit, n_dp)),
            dma((chunks, D_PARTS, n_dp)), dma((chunks, D_PARTS, n_dp)),
            dma((n_mp,)), dma((n_mp,)),
            dma((examples, n_mp)), dma((examples, n_mp)),
            dma, dma((n_sec,)),
            dma((group,)), dma((group,)),
            dma((n_sec,)), dma,
        ],
        compiler_params=pltpu.CompilerParams(
            collective_id=0, has_side_effects=True, vmem_limit_bytes=64 * 1024 * 1024
        ),
        cost_estimate=pl.CostEstimate(
            flops=2 * tokens * piece * width, bytes_accessed=2 * piece * w_cols, transcendentals=0
        ),
    )(cotangent, saved_inputs, pre_acts, weights, jnp.swapaxes(proj_in, 1, 2),
      jnp.swapaxes(proj_out, 1, 2), query_panels, partners)
    return pl.pallas_call(
        hand_over_kernel,
        out_shape=results,
        in_specs=[hbm, hbm],
        out_specs=(hbm, hbm),
        scratch_shapes=[dma((2,))],
        compiler_params=pltpu.CompilerParams(vmem_limit_bytes=64 * 1024 * 1024),
    )(*made)


def solution(mesh):
    placed = (
        P("dp", "mp"),
        P("section", "dp", "mp"),
        P("section", "dp", "mp"),
        P("section", "mp", "dp"),
        P("section", "mp", None),
        P("section", "mp", None),
        P("section", "dp", "mp"),
        P(),
    )
    sizes = (mesh.shape["section"], mesh.shape["dp"], mesh.shape["mp"])
    return jax.shard_map(
        functools.partial(body, sizes), mesh=mesh, in_specs=placed,
        out_specs=(P("section", "dp", "mp"), P()), check_vma=False,
    )
```

```python
import functools
import math

import jax
import jax.numpy as jnp
from jax import lax
from jax.experimental import pallas as pl
from jax.experimental.pallas import tpu as pltpu
from jax.sharding import PartitionSpec as P

LEN = 32
CHUNK = 16
W_PARTS = 4
MESH = pl.DeviceIdType.MESH


def ring(index, offset, count):
    return lax.rem(index + offset, count)


def dot_t(left, right):
    return lax.dot_general(
        left, right, (((1,), (1,)), ((), ())), preferred_element_type=jnp.float32
    )


def pack(block):
    half = block.shape[0] // 2
    return jnp.concatenate([block[:half], block[half:]], axis=1)


def unpack(block):
    half = block.shape[1] // 2
    return jnp.concatenate([block[:, :half], block[:, half:]], axis=0)


def relay_kernel(
    sizes, cot_hbm, inputs_hbm, pre_hbm, weights, proj_in_hbm, proj_out_hbm, queries_hbm, partners,
    panels, table,
    cot, inputs, pre, w_here, proj_in, proj_wide, queries,
    g_own, g_all, d_own, d_in, d_out, slope, in_slots, out_slots, in_wide, q_all, q_pad, spread_out, mask,
    layer_slots, section_slots, total, result,
    load, q_send, q_recv, g_send, g_recv, d_send, d_recv,
    in_send, in_recv, out_send, out_recv, a_send, a_recv, b_send, b_recv, c_send, c_recv,
):
    n_sec, n_dp, n_mp = sizes
    sec = lax.axis_index("section")
    dp = lax.axis_index("dp")
    mp = lax.axis_index("mp")
    tokens, piece = cot.shape
    loads = [
        pltpu.make_async_copy(src, dst, load.at[at])
        for at, (src, dst) in enumerate((
            (pre_hbm.at[0], pre), (cot_hbm, cot), (inputs_hbm.at[0], inputs),
            (proj_in_hbm.at[0], proj_in), (queries_hbm.at[0], queries),
            (proj_out_hbm.at[0], proj_wide.at[pl.ds(0, proj_out_hbm.shape[1])]), (weights.at[0], w_here),
        ))
    ]
    for copy in loads[:-1]:
        copy.start()
    load_pre, load_cot, load_inputs, load_in, load_queries, load_out, load_w = loads
    chunks = tokens // CHUNK
    rank = proj_in.shape[0]
    examples = tokens // LEN
    piece_rank = rank // n_mp
    asked = queries.shape[0]
    rounds = partners.shape[0]
    w_cols = w_here.shape[1]
    w_rows = w_here.shape[0] // W_PARTS
    unit = min(piece, w_cols)
    top = n_sec - 1
    group = n_dp * n_mp
    here = dp * n_mp + mp

    barrier = pltpu.get_barrier_semaphore()
    for off in range(1, group):
        other = ring(here, off, group)
        pl.semaphore_signal(
            barrier, inc=1,
            device_id={"section": sec, "dp": other // n_mp, "mp": lax.rem(other, n_mp)},
            device_id_type=MESH,
        )
    for off in range(1, n_sec):
        pl.semaphore_signal(
            barrier, inc=1,
            device_id={"section": ring(sec, off, n_sec), "dp": dp, "mp": mp},
            device_id_type=MESH,
        )
    for step in (1, n_sec - 1):
        for off in range(1, n_dp):
            pl.semaphore_signal(
                barrier, inc=1,
                device_id={
                    "section": ring(sec, step, n_sec), "dp": ring(dp, off, n_dp), "mp": mp
                },
                device_id_type=MESH,
            )

    def to(section, dp_at, mp_at, src, dst, send_sem, recv_sem):
        return pltpu.make_async_remote_copy(
            src_ref=src, dst_ref=dst, send_sem=send_sem, recv_sem=recv_sem,
            device_id={"section": section, "dp": dp_at, "mp": mp_at}, device_id_type=MESH,
        )

    def q_copy(off):
        return to(sec, ring(dp, off, n_dp), mp, queries, q_all.at[dp],
                  q_send.at[off], q_recv.at[off])

    def g_target(sub):
        column = mp * piece + sub * unit
        return column // w_cols, lax.rem(column, w_cols) // unit

    def g_source(at):
        return (dp * w_cols + at * unit) // piece

    def g_spot(chunk, source_dp, at):
        return g_all.at[
            chunk, pl.ds(pl.multiple_of(source_dp * CHUNK, CHUNK), CHUNK),
            pl.ds(pl.multiple_of(at * unit, unit), unit),
        ]

    def g_copy(chunk, sub, off):
        rows = pl.ds(pl.multiple_of(chunk * CHUNK, CHUNK), CHUNK)
        target, at = g_target(sub)
        return to(sec, target, ring(mp, off, n_mp), g_own.at[rows, sub * unit:(sub + 1) * unit],
                  g_spot(chunk, dp, at), g_send.at[chunk, sub, off], g_recv.at[chunk, at, dp])

    def g_move(chunk, act):
        for sub in range(piece // unit):
            target, _ = g_target(sub)
            for off in sorted(range(1, n_mp), key=lambda off: abs(2 * off - n_mp)):
                act(g_copy(chunk, sub, off))

            @pl.when(target != dp)
            def _():
                act(g_copy(chunk, sub, 0))

    def g_send_all(chunk):
        g_move(chunk, lambda copy: copy.start())
        rows = pl.ds(pl.multiple_of(chunk * CHUNK, CHUNK), CHUNK)
        for sub in range(piece // unit):
            target, at = g_target(sub)

            @pl.when(target == dp)
            def _():
                g_spot(chunk, dp, at)[...] = g_own[rows, sub * unit:(sub + 1) * unit]

    def g_arrival(chunk, source_dp, at):
        spot = g_spot(chunk, source_dp, at)
        return to(sec, dp, mp, spot, spot, g_send.at[chunk, 0, 0], g_recv.at[chunk, at, source_dp])

    def g_wait(chunk):
        for at in range(w_cols // unit):
            source = g_source(at)
            for off in range(n_dp):
                source_dp = ring(dp, off, n_dp)
                arrival = g_arrival(chunk, source_dp, at)
                if off:
                    arrival.wait_recv()
                else:
                    pl.when(source != mp)(arrival.wait_recv)

    def d_copy(chunk, target):
        rows = pl.ds(pl.multiple_of(chunk * CHUNK, CHUNK), CHUNK)
        return to(ring(sec, n_sec - 1, n_sec), target, mp,
                  d_out.at[chunk, target * CHUNK:(target + 1) * CHUNK], d_in.at[dp, rows],
                  d_send.at[chunk, target], d_recv.at[chunk, dp])

    def d_arrival(chunk, source):
        rows = pl.ds(pl.multiple_of(chunk * CHUNK, CHUNK), CHUNK)
        spot = d_in.at[source, rows]
        return to(sec, dp, mp, spot, spot, d_send.at[chunk, 0], d_recv.at[chunk, source])

    def in_copy(off):
        return to(sec, dp, ring(mp, off, n_mp), in_slots.at[0], in_slots.at[off],
                  in_send.at[off], in_recv.at[off])

    def out_copy(example, off):
        return to(sec, dp, ring(mp, off, n_mp), out_slots.at[0, example], out_slots.at[off, example],
                  out_send.at[example, off], out_recv.at[example, off])

    def a_copy():
        return to(0, dp, mp, total, layer_slots.at[sec], a_send, a_recv.at[sec])

    def b_copy(off):
        other = ring(here, off, group)
        return to(sec, other // n_mp, lax.rem(other, n_mp), section_slots.at[here],
                  section_slots.at[here], b_send.at[off], b_recv.at[off])

    def c_copy(section):
        return to(section, dp, mp, result, result, c_send.at[section], c_recv)

    def set_slopes(rows):
        value = pre[rows, :].astype(jnp.float32)
        sigma = 1.0 / (1.0 + jnp.exp(-value))
        slope[rows, :] = sigma * (1.0 + value * (1.0 - sigma))

    load_pre.wait()
    load_cot.wait()
    load_w.start()
    pl.semaphore_wait(barrier, group - 1 + n_sec - 1 + 2 * (n_dp - 1))

    @pl.when(sec < top)
    def _():
        set_slopes(slice(0, tokens))

    q_row = lax.broadcasted_iota(jnp.int32, total.shape, 0)
    r_lane = lax.broadcasted_iota(jnp.int32, total.shape, 1)

    def prepare():
        load_queries.wait()
        q_all[dp] = queries[...]
        for off in range(1, n_dp):
            q_copy(off).start()

        load_inputs.wait()
        load_in.wait()
        in_slots[0] = pack(dot_t(inputs[...], proj_in[...]))
        for off in range(1, n_mp):
            in_copy(off).start()

        spread = spread_out.shape
        spread_row = lax.broadcasted_iota(jnp.int32, spread, 0)
        spread_col = lax.broadcasted_iota(jnp.int32, spread, 1)
        spread_out[...] = (spread_row == spread_col % rank).astype(jnp.bfloat16)
        spread_in = (
            spread_row[:rank] == mp * piece_rank + spread_col[:rank] // rank
        ).astype(jnp.bfloat16)

        chosen = jnp.zeros(total.shape, jnp.float32)
        for round_at in range(rounds):
            for index in range(n_dp):
                spot = jnp.logical_and(q_row // asked == index, r_lane // examples == round_at)
                hit = jnp.where(partners[round_at, index] == dp, 1.0, 0.0).astype(jnp.float32)
                chosen = chosen + jnp.where(spot, hit, 0.0)
        mask[...] = chosen * (1.0 / (rank * math.sqrt(n_sec)))
        total[...] = jnp.zeros_like(total)

        q_pad[...] = jnp.zeros_like(q_pad)
        for off in range(1, n_dp):
            q_copy(off).wait_recv()
        for index in range(n_dp):
            q_pad[index * asked:(index + 1) * asked, :] = q_all[index]

        for off in range(1, n_mp):
            in_copy(off).wait_recv()
        in_side = in_slots[0]
        for off in range(1, n_mp):
            in_side = in_side + in_slots[off]
        in_side = unpack(in_side) * (1.0 / math.sqrt(LEN))
        in_high = in_side.astype(jnp.bfloat16)
        in_low = (in_side - in_high.astype(jnp.float32)).astype(jnp.bfloat16)
        in_wide[...] = (
            jnp.dot(in_high, spread_in, preferred_element_type=jnp.float32)
            + jnp.dot(in_low, spread_in, preferred_element_type=jnp.float32)
        )

    def step_rows(chunk):
        return pl.ds(pl.multiple_of(chunk * CHUNK, CHUNK), CHUNK)

    def open_top(chunk):
        rows = step_rows(chunk)
        set_slopes(rows)
        d_own[rows, :] = cot[rows, :]
        g_own[rows, :] = (cot[rows, :].astype(jnp.float32) * slope[rows, :]).astype(jnp.bfloat16)

    def take(chunk):
        rows = step_rows(chunk)
        delta = jnp.zeros((CHUNK, piece), jnp.float32)
        for source in range(n_dp):
            d_arrival(chunk, source).wait_recv()
            delta = delta + d_in[source, rows, :].astype(jnp.float32)
        delta = delta.astype(jnp.bfloat16)
        d_own[rows, :] = delta
        g_own[rows, :] = (delta.astype(jnp.float32) * slope[rows, :]).astype(jnp.bfloat16)

    def multiply(chunk):
        rows = step_rows(chunk)
        g_wait(chunk)
        for part in range(W_PARTS):
            cols = slice(part * w_rows, (part + 1) * w_rows)
            back = dot_t(w_here[cols, :], g_all[chunk]).T
            delta = d_own[rows, cols].astype(jnp.float32)
            for target in range(n_dp):
                at = slice(target * CHUNK, (target + 1) * CHUNK)
                d_out[chunk, at, cols] = (
                    back[at] + jnp.where(dp == target, delta, 0.0)
                ).astype(jnp.bfloat16)
        for target in range(n_dp):
            d_copy(chunk, target).start()

    def project(example):
        rows = pl.ds(pl.multiple_of(example * LEN, LEN), LEN)
        out_slots[0, example] = dot_t(g_own[rows, :], proj_wide[...]).astype(jnp.bfloat16)
        for off in range(1, n_mp):
            out_copy(example, off).start()

    per = LEN // CHUNK

    def panel(example):
        out_side = jnp.zeros((LEN, out_slots.shape[3]), jnp.float32)
        for off in range(n_mp):
            if off:
                out_copy(example, off).wait_recv()
            out_side = out_side + out_slots[off, example].astype(jnp.float32)
        out_wide = jnp.dot(
            out_side.astype(jnp.bfloat16), spread_out[...], preferred_element_type=jnp.float32
        )
        rows = pl.ds(pl.multiple_of(example * LEN, LEN), LEN)
        row = jnp.sum(in_wide[rows, :] * out_wide, axis=0, keepdims=True)
        panels[0, pl.ds(example, 1), :] = row
        column = jnp.sum(q_pad[...] * row, axis=1, keepdims=True)
        total[...] += jnp.where(lax.rem(r_lane, examples) == example, column, 0.0)

    proj_wide[rank:, :] = jnp.zeros((proj_wide.shape[0] - rank, piece), jnp.bfloat16)
    load_out.wait()
    pl.when(sec < top)(prepare)

    @pl.when(sec > 0)
    def _():
        @pl.loop(0, chunks + 1)
        def _(step):
            pl.when(step == 1)(load_w.wait)

            @pl.when(step < chunks)
            def _():
                @pl.when(sec == top)
                def _():
                    open_top(step)

                @pl.when(sec < top)
                def _():
                    take(step)

                g_send_all(step)

            @pl.when(step > 0)
            def _():
                multiply(step - 1)

                @pl.when(lax.rem(step, per) == 0)
                def _():
                    project(step // per - 1)

        pl.when(sec == top)(prepare)

        @pl.loop(0, examples)
        def _(example):
            panel(example)

    @pl.when(sec == 0)
    def _():
        load_w.wait()

        @pl.loop(0, chunks)
        def _(step):
            take(step)

            @pl.when(lax.rem(step, per) == per - 1)
            def _():
                project(step // per)

                @pl.when(step >= per)
                def _():
                    panel(step // per - 1)

        panel(examples - 1)

    share = total[...] * mask[...]

    @pl.when(sec > 0)
    def _():
        total[...] = share
        copy = a_copy()
        copy.start()
        copy.wait_send()
        c_copy(sec).wait_recv()

    @pl.when(sec == 0)
    def _():
        summed = share
        for section in range(1, n_sec):
            to(0, dp, mp, total, layer_slots.at[section], a_send, a_recv.at[section]).wait_recv()
            summed = summed + layer_slots[section]
        section_slots[here] = summed
        for off in range(1, group):
            b_copy(off).start()
        for off in range(1, group):
            b_copy(off).wait_recv()
        all_parts = section_slots[0]
        for slot in range(1, group):
            all_parts = all_parts + section_slots[slot]
        result[...] = all_parts
        for section in range(1, n_sec):
            c_copy(section).start()
        for off in range(1, group):
            b_copy(off).wait_send()
        for section in range(1, n_sec):
            c_copy(section).wait_send()

    for query in range(n_dp * asked):
        for round_at in range(rounds):
            table[query, round_at:round_at + 1, :] = result[
                query:query + 1, round_at * examples:(round_at + 1) * examples
            ]

    for off in range(1, n_dp):
        q_copy(off).wait_send()
    for off in range(1, n_mp):
        in_copy(off).wait_send()

    @pl.loop(0, examples)
    def _(example):
        for off in range(1, n_mp):
            out_copy(example, off).wait_send()

    @pl.when(sec > 0)
    def _():
        @pl.loop(0, chunks)
        def _(chunk):
            g_move(chunk, lambda copy: copy.wait_send())
            for target in range(n_dp):
                d_copy(chunk, target).wait_send()


def hand_over_kernel(panels, table, panels_out, table_out, done):
    copies = [
        pltpu.make_async_copy(panels, panels_out, done.at[0]),
        pltpu.make_async_copy(table, table_out, done.at[1]),
    ]
    for copy in copies:
        copy.start()
    for copy in copies:
        copy.wait()


def body(sizes, cotangent, saved_inputs, pre_acts, weights, proj_in, proj_out, query_panels, partners):
    n_sec, n_dp, n_mp = sizes
    tokens, piece = cotangent.shape
    width = piece * n_mp
    w_cols = weights.shape[2]
    unit = min(piece, w_cols)
    rank = proj_in.shape[2]
    examples = tokens // LEN
    asked = query_panels.shape[1]
    rounds = partners.shape[0]
    chunks = tokens // CHUNK
    panel = query_panels.shape[2]
    q_rows = -(-(n_dp * asked) // 8) * 8
    lanes = 128
    group = n_dp * n_mp
    dma = pltpu.SemaphoreType.DMA
    vmem = pl.BlockSpec(memory_space=pltpu.VMEM)
    hbm = pl.BlockSpec(memory_space=pltpu.HBM)
    results = (
        jax.ShapeDtypeStruct((1, examples, panel), jnp.float32),
        jax.ShapeDtypeStruct((n_dp * asked, rounds, examples), jnp.float32),
    )
    made = pl.pallas_call(
        functools.partial(relay_kernel, sizes),
        out_shape=results,
        in_specs=[hbm] * 7 + [pl.BlockSpec(memory_space=pltpu.SMEM)],
        out_specs=(vmem, vmem),
        scratch_shapes=[
            pltpu.VMEM((tokens, piece), jnp.bfloat16),
            pltpu.VMEM((tokens, piece), jnp.bfloat16),
            pltpu.VMEM((tokens, piece), jnp.bfloat16),
            pltpu.VMEM((piece, w_cols), jnp.bfloat16),
            pltpu.VMEM((rank, piece), jnp.bfloat16),
            pltpu.VMEM((2 * rank, piece), jnp.bfloat16),
            pltpu.VMEM((asked, panel), jnp.float32),
            pltpu.VMEM((tokens, piece), jnp.bfloat16),
            pltpu.VMEM((chunks, n_dp * CHUNK, w_cols), jnp.bfloat16),
            pltpu.VMEM((tokens, piece), jnp.bfloat16),
            pltpu.VMEM((n_dp, tokens, piece), jnp.bfloat16),
            pltpu.VMEM((chunks, n_dp * CHUNK, piece), jnp.bfloat16),
            pltpu.VMEM((tokens, piece), jnp.float32),
            pltpu.VMEM((n_mp, tokens // 2, 2 * rank), jnp.float32),
            pltpu.VMEM((n_mp, examples, LEN, 2 * rank), jnp.bfloat16),
            pltpu.VMEM((tokens, panel), jnp.float32),
            pltpu.VMEM((n_dp, asked, panel), jnp.float32),
            pltpu.VMEM((q_rows, panel), jnp.float32),
            pltpu.VMEM((2 * rank, panel), jnp.bfloat16),
            pltpu.VMEM((q_rows, lanes), jnp.float32),
            pltpu.VMEM((n_sec, q_rows, lanes), jnp.float32),
            pltpu.VMEM((group, q_rows, lanes), jnp.float32),
            pltpu.VMEM((q_rows, lanes), jnp.float32),
            pltpu.VMEM((q_rows, lanes), jnp.float32),
            dma((7,)),
            dma((n_dp,)), dma((n_dp,)),
            dma((chunks, piece // unit, n_mp)), dma((chunks, w_cols // unit, n_dp)),
            dma((chunks, n_dp)), dma((chunks, n_dp)),
            dma((n_mp,)), dma((n_mp,)),
            dma((examples, n_mp)), dma((examples, n_mp)),
            dma, dma((n_sec,)),
            dma((group,)), dma((group,)),
            dma((n_sec,)), dma,
        ],
        compiler_params=pltpu.CompilerParams(
            collective_id=0, has_side_effects=True, vmem_limit_bytes=64 * 1024 * 1024
        ),
        cost_estimate=pl.CostEstimate(
            flops=2 * tokens * piece * width, bytes_accessed=2 * piece * w_cols, transcendentals=0
        ),
    )(cotangent, saved_inputs, pre_acts, weights, jnp.swapaxes(proj_in, 1, 2),
      jnp.swapaxes(proj_out, 1, 2), query_panels, partners)
    return pl.pallas_call(
        hand_over_kernel,
        out_shape=results,
        in_specs=[hbm, hbm],
        out_specs=(hbm, hbm),
        scratch_shapes=[dma((2,))],
        compiler_params=pltpu.CompilerParams(vmem_limit_bytes=64 * 1024 * 1024),
    )(*made)


def solution(mesh):
    placed = (
        P("dp", "mp"),
        P("section", "dp", "mp"),
        P("section", "dp", "mp"),
        P("section", "mp", "dp"),
        P("section", "mp", None),
        P("section", "mp", None),
        P("section", "dp", "mp"),
        P(),
    )
    sizes = (mesh.shape["section"], mesh.shape["dp"], mesh.shape["mp"])
    return jax.shard_map(
        functools.partial(body, sizes), mesh=mesh, in_specs=placed,
        out_specs=(P("section", "dp", "mp"), P()), check_vma=False,
    )
```
